256 devices in a mesh: wide: 32 (over y, x, core), narrow: 8 (over z).
Axes of the slice: x: 4, y: 4, z: 8, core: 2. Of those that a mesh axis runs over, the one named last changes fastest.
Arguments:
- section_state: bfloat16 [24, 4096, 4096], P(None, 'wide', 'narrow'), may hold values from -6 to 6
- cotangent: bfloat16 [24, 4096, 4096], P(None, 'wide', 'narrow'), may hold values from -6 to 6
- bypass_weight: bfloat16 [24, 24], replicated, may hold values from -1.25 to 1.25
- bias: float32 [24], replicated, may hold values from -3 to 3
- spectral_weight: float32 [2, 24, 24, 4096], P(None, None, None, ('wide', 'narrow')), may hold values from -36 to 36
Outputs:
- section_slope: bfloat16 [24, 4096, 4096], P(None, 'wide', 'narrow')
- state_grad: bfloat16 [24, 4096, 4096], P(None, 'wide', 'narrow')
- weight_grad: float32 [2, 24, 24, 4096], P(None, None, None, ('wide', 'narrow'))
The draws below stay inside these ranges and needn't reach their ends.
All inputs are finite; a program needn't handle non-finite values.
Results may differ from the reference program's by a relative error of at most 0.007.
Values sent between devices are 32-bit elements; how exact they have to be, the bound alone decides.
A program may use at most 128 MiB of HBM per device.

```python
import math
import jax
import jax.numpy as jnp
from jax import lax

GRID = 4096
C = 24
MX = 64
MY = 64
MODES = 4096


def steps_of(rng, shape, cuts, least, top_value):
    factor_of = 1.0
    for position, shards_of in cuts:
        steps = jax.random.uniform(jax.random.fold_in(jax.random.fold_in(rng, 6), position), (shards_of,), jnp.float32, least / len(cuts), top_value / len(cuts))
        factor_of = factor_of * jnp.repeat(jnp.exp(steps), shape[position] // shards_of).reshape((-1,) + (1,) * (len(shape) - 1 - position))
    return factor_of


def gaussian(key, dims, scale, reach, shards=(), kind=jnp.bfloat16):
    loudness = steps_of(key, dims, shards, -0.22, 0.18) if shards else 1.0
    drawn = jax.random.normal(key, dims, jnp.float32) * scale * loudness
    return jnp.minimum(jnp.maximum(drawn, -reach), reach).astype(kind)


def setup_inputs(seed: int = 0) -> dict:
    seeds = jax.random.split(jax.random.key(seed), 6)
    section_state = gaussian(seeds[0], (C, GRID, GRID), 1.0, 6.0, ((1, 32), (2, 8)))
    cotangent = gaussian(seeds[1], (C, GRID, GRID), 1.0, 6.0, ((1, 32), (2, 8)))
    bypass_weight = gaussian(seeds[2], (C, C), C ** -0.5, 1.25)
    bias = gaussian(seeds[3], (C,), 0.5, 3.0, (), jnp.float32)
    spectral_weight = gaussian(seeds[4], (2, C, C, MODES), 6.0, 36.0, ((3, 256),), jnp.float32)
    return {"section_state": section_state, "cotangent": cotangent, "bypass_weight": bypass_weight, "bias": bias, "spectral_weight": spectral_weight}


PRECISE = lax.Precision.HIGHEST

def tables(frequency, positions):
    phases = jnp.mod(frequency[:, None] * positions[None, :], GRID).astype(jnp.float32) * (2.0 * math.pi / GRID)
    return (jnp.cos(phases), jnp.sin(phases))

def row_tables(first_row, span_len):
    counter = jnp.arange(MX, dtype=jnp.int32)
    frequency = jnp.where(counter < MX // 2, counter, counter - MX)
    return tables(frequency, first_row + jnp.arange(span_len, dtype=jnp.int32))

def column_basis(first_col, span_len):
    cos_y, sin_y = tables(jnp.arange(MY, dtype=jnp.int32), first_col + jnp.arange(span_len, dtype=jnp.int32))
    return jnp.concatenate([cos_y, sin_y], axis=0).T.astype(jnp.bfloat16)

def mode_weight():
    return jnp.where(jnp.arange(MY) == 0, 1.0, 2.0).astype(jnp.float32)

def contract(table, values):
    return jnp.einsum('kx,cxm->ckm', table, values, precision=PRECISE)

def spread(table, values):
    return jnp.einsum('kx,ckm->cxm', table, values, precision=PRECISE)

def to_columns(tile_data, col_basis):
    channels, tile_rows, tile_cols = tile_data.shape
    product = jnp.dot(tile_data.reshape(channels * tile_rows, tile_cols), col_basis, preferred_element_type=jnp.float32)
    return product.reshape(channels, tile_rows, 2 * MY)

def from_columns(halves, col_basis):
    channels, tile_rows, width = halves.shape
    product = lax.dot_general(halves.reshape(channels * tile_rows, width), col_basis, (((1,), (1,)), ((), ())), preferred_element_type=jnp.float32)
    return product.reshape(channels, tile_rows, col_basis.shape[0])

def spectrum_part(halves, cos_x, sin_x):
    channels = halves.shape[0]
    first_half = halves[..., :MY]
    second_half = halves[..., MY:]
    real_part = contract(cos_x, first_half) - contract(sin_x, second_half)
    imag_part = -(contract(sin_x, first_half) + contract(cos_x, second_half))
    return jnp.stack([real_part.reshape(channels, MX * MY), imag_part.reshape(channels, MX * MY)]) / GRID

def cotangent_part(halves, cos_x, sin_x):
    channels = halves.shape[0]
    weight = mode_weight()
    first_half = weight * halves[..., :MY]
    second_half = -weight * halves[..., MY:]
    real_part = contract(cos_x, first_half) + contract(sin_x, second_half)
    imag_part = contract(cos_x, second_half) - contract(sin_x, first_half)
    return jnp.stack([real_part.reshape(channels, MX * MY), imag_part.reshape(channels, MX * MY)])

def mix(weights, spectrum):
    w_real, w_imag = (weights[0], weights[1])
    x_real, x_imag = (spectrum[0], spectrum[1])
    real_part = jnp.einsum('iom,im->om', w_real, x_real, precision=PRECISE) - jnp.einsum('iom,im->om', w_imag, x_imag, precision=PRECISE)
    imag_part = jnp.einsum('iom,im->om', w_real, x_imag, precision=PRECISE) + jnp.einsum('iom,im->om', w_imag, x_real, precision=PRECISE)
    return jnp.stack([real_part, imag_part])

def mix_back(weights, cot_modes):
    w_real, w_imag = (weights[0], weights[1])
    y_real, y_imag = (cot_modes[0], cot_modes[1])
    real_part = jnp.einsum('iom,om->im', w_real, y_real, precision=PRECISE) + jnp.einsum('iom,om->im', w_imag, y_imag, precision=PRECISE)
    imag_part = jnp.einsum('iom,om->im', w_real, y_imag, precision=PRECISE) - jnp.einsum('iom,om->im', w_imag, y_real, precision=PRECISE)
    return jnp.stack([real_part, imag_part])

def weight_terms(spectrum, cot_modes):
    x_real, x_imag = (spectrum[0], spectrum[1])
    y_real, y_imag = (cot_modes[0], cot_modes[1])
    real_part = jnp.einsum('im,om->iom', x_real, y_real, precision=PRECISE) + jnp.einsum('im,om->iom', x_imag, y_imag, precision=PRECISE)
    imag_part = jnp.einsum('im,om->iom', x_real, y_imag, precision=PRECISE) - jnp.einsum('im,om->iom', x_imag, y_real, precision=PRECISE)
    return jnp.stack([real_part, imag_part])

def expand_rows(modes, cos_x, sin_x):
    channels = modes.shape[1]
    real_part = modes[0].reshape(channels, MX, MY)
    imag_part = modes[1].reshape(channels, MX, MY)
    first_half = spread(cos_x, real_part) - spread(sin_x, imag_part)
    second_half = spread(sin_x, real_part) + spread(cos_x, imag_part)
    weight = mode_weight()
    return jnp.concatenate([weight * first_half, -weight * second_half], axis=-1).astype(jnp.bfloat16)

def expand_back(modes, cos_x, sin_x):
    channels = modes.shape[1]
    real_part = modes[0].reshape(channels, MX, MY)
    imag_part = modes[1].reshape(channels, MX, MY)
    first_half = (spread(cos_x, real_part) - spread(sin_x, imag_part)) / GRID
    second_half = (-spread(sin_x, real_part) - spread(cos_x, imag_part)) / GRID
    return jnp.concatenate([first_half, second_half], axis=-1).astype(jnp.bfloat16)

def gelu_slope(values):
    return 0.5 * (1.0 + jax.scipy.special.erf(values * (1.0 / math.sqrt(2.0)))) + values * jnp.exp(-0.5 * values * values) * (1.0 / math.sqrt(2.0 * math.pi))

def reference(section_state, cotangent, bypass_weight, bias, spectral_weight):
    channels = section_state.shape[0]
    cos_x, sin_x = row_tables(0, GRID)
    col_basis = column_basis(0, GRID)
    spectrum = spectrum_part(to_columns(section_state, col_basis), cos_x, sin_x)
    mixed_modes = mix(spectral_weight, spectrum)
    spectral = from_columns(expand_rows(mixed_modes, cos_x, sin_x), col_basis) / GRID
    bypass = lax.dot_general(bypass_weight, section_state.reshape(channels, -1), (((0,), (0,)), ((), ())), preferred_element_type=jnp.float32).reshape(section_state.shape)
    pre_act = bypass + spectral + bias[:, None, None]
    section_slope = jax.nn.gelu(pre_act, approximate=False).astype(jnp.bfloat16)
    seed_grad = (cotangent.astype(jnp.float32) * gelu_slope(pre_act)).astype(jnp.bfloat16)
    direct = jnp.dot(bypass_weight, seed_grad.reshape(channels, -1), preferred_element_type=jnp.float32).reshape(section_state.shape)
    cot_modes = cotangent_part(to_columns(seed_grad, col_basis) / GRID, cos_x, sin_x)
    weight_grad = weight_terms(spectrum, cot_modes)
    pulled = mix_back(spectral_weight, cot_modes)
    state_grad = (direct + from_columns(expand_back(pulled, cos_x, sin_x), col_basis)).astype(jnp.bfloat16)
    return (section_slope, state_grad, weight_grad)
```

```python
import math

import jax
import jax.numpy as jnp
import ml_dtypes
import numpy as np
from jax import lax
from jax.experimental import pallas as pl
from jax.experimental.pallas import tpu as pltpu
from jax.sharding import PartitionSpec as P

GRID = 4096
C = 24
MX = 64
MY = 64
WIDE = 32
NARROW = 8
PLANE = 16
ROWS = GRID // WIDE
COLS = GRID // NARROW
GROUPS = C // 8
SLAB = 16
MESH = pl.DeviceIdType.MESH
F32 = jnp.float32
BF16 = jnp.bfloat16


def split_np(values):
    high = values.astype(ml_dtypes.bfloat16)
    low = (values - high.astype(np.float64)).astype(ml_dtypes.bfloat16)
    return high, low


def column_tables():
    m = np.arange(MY)
    phase = (m[None, :] * np.arange(GRID)[:, None]) % GRID * (2.0 * math.pi / GRID)
    cos_y = np.cos(phase).astype(np.float32).reshape(GRID, 4, 1, 16)
    sin_y = np.sin(phase).astype(np.float32).reshape(GRID, 4, 1, 16)
    with_cos = np.concatenate([cos_y, -sin_y], axis=2).reshape(GRID, 128)
    with_sin = np.concatenate([-sin_y, -cos_y], axis=2).reshape(GRID, 128)
    basis = np.concatenate([with_cos, with_sin], axis=1).astype(ml_dtypes.bfloat16)
    basis = basis.reshape(NARROW, COLS, 256)
    return basis, np.ascontiguousarray(basis.transpose(0, 2, 1))


def row_tables():
    r = np.arange(MX)
    core, plane, low = r // 32, (r // 2) % 16, r % 2
    k = 4 * plane + 2 * core + low
    freq = np.where(k < MX // 2, k, k - MX)
    phase = (freq[:, None] * np.arange(GRID)[None, :]) % GRID * (2.0 * math.pi / GRID)
    cos_x = np.cos(phase).reshape(MX, WIDE, ROWS).transpose(1, 0, 2)
    sin_x = np.sin(phase).reshape(MX, WIDE, ROWS).transpose(1, 0, 2)
    both = np.concatenate([cos_x, sin_x], axis=2)
    high, low = split_np(both)
    down = np.concatenate([high, low], axis=1).astype(np.float64) / GRID
    down = down.astype(ml_dtypes.bfloat16)
    high_t, low_t = high.transpose(0, 2, 1), low.transpose(0, 2, 1)
    up = np.ascontiguousarray(np.concatenate([high_t, high_t, low_t], axis=2))
    return down, up


def split(values):
    high = values.astype(BF16)
    return high, (values - high.astype(F32)).astype(BF16)


def dot(a, b):
    return jnp.dot(a, b, preferred_element_type=F32)


def rows_down(part, down, store):
    stacked = jnp.concatenate([part[:, :128], part[:, 128:]], axis=0)
    high, low = split(stacked)
    four = dot(down, jnp.concatenate([high, low], axis=1))
    store(four[:64, :128] + (four[:64, 128:] + four[64:, :128]))


def lanes():
    return lax.broadcasted_iota(jnp.int32, (8, 128), 1)


def roll(tile, shift):
    return pltpu.roll(tile, shift % 128, 1)


def place():
    wide = lax.axis_index("wide")
    z = lax.axis_index("narrow")
    return lax.div(wide, 2), lax.rem(wide, 2), z


def greet():
    plane, core, z = place()
    barrier = pltpu.get_barrier_semaphore()

    def to_plane(d, carry):
        t = lax.rem(plane + d, PLANE)
        pl.semaphore_signal(barrier, inc=1, device_id=(t * 2 + core, z), device_id_type=MESH)
        return carry

    def to_ring(d, carry):
        t = lax.rem(z + d, NARROW)
        pl.semaphore_signal(
            barrier, inc=1, device_id=(plane * 2 + core, t), device_id_type=MESH
        )
        return carry

    pl.semaphore_signal(
        barrier, inc=1, device_id=(plane * 2 + 1 - core, z), device_id_type=MESH
    )
    lax.fori_loop(1, PLANE, to_plane, 0)
    lax.fori_loop(1, NARROW, to_ring, 0)


def greeted():
    pl.semaphore_wait(pltpu.get_barrier_semaphore(), 1 + (PLANE - 1) + (NARROW - 1))


def remote(src, dst, send, recv, wide, z):
    return pltpu.make_async_remote_copy(
        src_ref=src,
        dst_ref=dst,
        send_sem=send,
        recv_sem=recv,
        device_id=(wide, z),
        device_id_type=MESH,
    )


COMM_SCRATCH = [
    pltpu.VMEM((GROUPS, 256, 128), F32),
    pltpu.VMEM((GROUPS, PLANE, 16, 128), F32),
    pltpu.VMEM((NARROW, 8, 128), F32),
    pltpu.VMEM((NARROW, 8, 128), F32),
    pltpu.VMEM((8, 128), F32),
    pltpu.VMEM((NARROW, 8, 128), F32),
    pltpu.VMEM((MX * C, 128), F32),
    pltpu.SemaphoreType.DMA((2, GROUPS)),
    pltpu.SemaphoreType.DMA((2, GROUPS, PLANE)),
    pltpu.SemaphoreType.DMA((2, NARROW)),
    pltpu.SemaphoreType.DMA((2, NARROW)),
    pltpu.SemaphoreType.DMA((2, PLANE)),
    pltpu.SemaphoreType.DMA((2, PLANE)),
]


def pair_copy(parts, comm, g):
    plane, core, z = place()
    sems = comm[7]
    return remote(
        parts.at[g, 1 - core],
        comm[0].at[g],
        sems.at[0, g],
        sems.at[1, g],
        plane * 2 + 1 - core,
        z,
    )


def reduce_scatter(parts, comm):
    pair, slots, packed, ring = comm[:4]
    plane_sems, ring_sems = comm[8], comm[9]
    plane, core, z = place()

    def plane_copy(g, t, j):
        return remote(
            pair.at[g, pl.ds(pl.multiple_of(t * 16, 16), 16)],
            slots.at[g, j],
            plane_sems.at[0, g, t],
            plane_sems.at[1, g, j],
            t * 2 + core,
            z,
        )

    for g in range(GROUPS):
        pair_copy(parts, comm, g).wait_recv()
        pair[g] = pair[g] + parts[g, core]

        def send(d, carry, g=g):
            plane_copy(g, lax.rem(plane + d, PLANE), plane).start()
            return carry

        lax.fori_loop(1, PLANE, send, 0)
        slots[g, plane] = pair[g, pl.ds(pl.multiple_of(plane * 16, 16), 16)]

    sums = []
    for g in range(GROUPS):

        def arrive(d, carry, g=g):
            plane_copy(g, plane, lax.rem(plane + PLANE - d, PLANE)).wait_recv()
            return carry

        lax.fori_loop(1, PLANE, arrive, 0)
        sums.append(jnp.sum(slots[g], axis=0))

    lane_group = lanes() // 32
    for low in range(2):
        for quarter in range(4):
            tile = jnp.zeros((8, 128), F32)
            for g in range(GROUPS):
                moved = roll(sums[g][low * 8 : low * 8 + 8], 32 * (g - quarter))
                tile = jnp.where(lane_group == g, moved, tile)
            packed[low * 4 + quarter] = tile

    def ring_copy(t, j):
        return remote(
            packed.at[t], ring.at[j], ring_sems.at[0, t], ring_sems.at[1, j], plane * 2 + core, t
        )

    def ring_send(d, carry):
        ring_copy(lax.rem(z + d, NARROW), z).start()
        return carry

    def ring_arrive(d, carry):
        ring_copy(z, lax.rem(z + NARROW - d, NARROW)).wait_recv()
        return carry

    lax.fori_loop(1, NARROW, ring_send, 0)
    ring[z] = packed[z]
    lax.fori_loop(1, NARROW, ring_arrive, 0)
    total = jnp.sum(ring[...], axis=0)

    def sent_plane(d, carry):
        t = lax.rem(plane + d, PLANE)
        for g in range(GROUPS):
            plane_copy(g, t, plane).wait_send()
        return carry

    def sent_ring(d, carry):
        ring_copy(lax.rem(z + d, NARROW), z).wait_send()
        return carry

    for g in range(GROUPS):
        pair_copy(parts, comm, g).wait_send()
    lax.fori_loop(1, PLANE, sent_plane, 0)
    lax.fori_loop(1, NARROW, sent_ring, 0)
    return total


def pack(real, imag):
    pad = jnp.zeros((8, 96), F32)
    lane_group = lanes() // 32
    tile = jnp.zeros((8, 128), F32)
    for g in range(GROUPS):
        rows = slice(g * 8, g * 8 + 8)
        wide_tile = jnp.concatenate([real[rows], imag[rows], pad], axis=1)
        tile = jnp.where(lane_group == g, roll(wide_tile, 32 * g), tile)
    return tile


def all_gather(tile, comm):
    own, ring, modes = comm[4:7]
    ring_sems, plane_sems, pair_sems = comm[10:13]
    plane, core, z = place()
    own[...] = tile

    def ring_copy(t, j):
        return remote(
            own, ring.at[j], ring_sems.at[0, t], ring_sems.at[1, j], plane * 2 + core, t
        )

    def ring_send(d, carry):
        ring_copy(lax.rem(z + d, NARROW), z).start()
        return carry

    def ring_arrive(d, carry):
        ring_copy(z, lax.rem(z + NARROW - d, NARROW)).wait_recv()
        return carry

    lax.fori_loop(1, NARROW, ring_send, 0)
    ring[z] = tile
    lax.fori_loop(1, NARROW, ring_arrive, 0)

    def chunk(which, j):
        return modes.at[pl.ds(pl.multiple_of((which * PLANE + j) * 48, 48), 48)]

    lane_group = lanes() // 32
    blocks = []
    for low in range(2):
        for g in range(GROUPS):
            block = jnp.zeros((8, 128), F32)
            for quarter in range(4):
                moved = roll(ring[low * 4 + quarter], 32 * (quarter - g))
                block = jnp.where(lane_group == quarter, moved, block)
            blocks.append(block)
    modes[pl.ds(pl.multiple_of((core * PLANE + plane) * 48, 48), 48)] = jnp.concatenate(
        blocks, axis=0
    )

    def plane_copy(t, j):
        return remote(
            chunk(core, j), chunk(core, j), plane_sems.at[0, t], plane_sems.at[1, j], t * 2 + core, z
        )

    def pair_forward(which, j):
        return remote(
            chunk(which, j),
            chunk(which, j),
            pair_sems.at[0, j],
            pair_sems.at[1, j],
            plane * 2 + 1 - core,
            z,
        )

    def plane_send(d, carry):
        plane_copy(lax.rem(plane + d, PLANE), plane).start()
        return carry

    def plane_arrive(d, carry):
        j = lax.rem(plane + PLANE - d, PLANE)
        plane_copy(plane, j).wait_recv()
        pair_forward(core, j).start()
        return carry

    def pair_arrive(j, carry):
        pair_forward(1 - core, j).wait_recv()
        return carry

    def sent(d, carry):
        plane_copy(lax.rem(plane + d, PLANE), plane).wait_send()
        return carry

    def pair_sent(j, carry):
        pair_forward(core, j).wait_send()
        return carry

    def ring_sent(d, carry):
        ring_copy(lax.rem(z + d, NARROW), z).wait_send()
        return carry

    lax.fori_loop(1, PLANE, plane_send, 0)
    pair_forward(core, plane).start()
    lax.fori_loop(1, PLANE, plane_arrive, 0)
    lax.fori_loop(0, PLANE, pair_arrive, 0)
    lax.fori_loop(1, PLANE, sent, 0)
    lax.fori_loop(0, PLANE, pair_sent, 0)
    lax.fori_loop(1, NARROW, ring_sent, 0)


def expand(modes, up, out_ref):
    for c in range(0, C, 2):
        both = jnp.concatenate(
            [modes[pl.ds(c + i, MX, stride=C), :] for i in range(2)], axis=1
        )
        high, low = split(both)
        rows = dot(up, jnp.concatenate([high, low, high], axis=0))
        for i in range(2):
            at = slice(i * 128, i * 128 + 128)
            out_ref[c + i] = jnp.concatenate([rows[:128, at], rows[128:, at]], axis=1).astype(
                BF16
            )


def unpack(tile):
    real = [roll(tile, -32 * g) for g in range(GROUPS)]
    imag = [roll(tile, -32 * g - 16) for g in range(GROUPS)]
    return real, imag


def mode_weight():
    z = lax.axis_index("narrow")
    first = jnp.logical_and(lanes() % 16 == 0, lax.rem(z, 4) == 0)
    return jnp.where(first, 1.0, 2.0).astype(F32)


def forward_kernel(
    state_hbm, weights, basis_hbm, down_hbm, up_hbm, rows_out, spectrum_out, *scratch
):
    state, basis, down, up, parts, load_sems, *comm = scratch
    plane, core, z = place()
    wide = plane * 2 + core
    loads = [
        pltpu.make_async_copy(basis_hbm.at[z], basis, load_sems.at[0]),
        pltpu.make_async_copy(down_hbm.at[wide], down, load_sems.at[1]),
        pltpu.make_async_copy(up_hbm.at[wide], up, load_sems.at[2]),
    ]
    for g in range(GROUPS):
        at = pl.ds(g * 8, 8)
        loads.append(pltpu.make_async_copy(state_hbm.at[at], state.at[at], load_sems.at[3 + g]))
    for load in loads:
        load.start()
    greet()
    for load in loads[:3]:
        load.wait()
    for g in range(GROUPS):
        loads[3 + g].wait()
        for row in range(8):
            part = dot(state[g * 8 + row], basis[...])

            def store(value, g=g, row=row):
                parts[g, 0, pl.ds(row, 32, stride=8), :] = value[:32]
                parts[g, 1, pl.ds(row, 32, stride=8), :] = value[32:]

            rows_down(part, down[...], store)
        if g == 0:
            greeted()
        pair_copy(parts, comm, g).start()
    spectrum = reduce_scatter(parts, comm)
    spectrum_out[...] = spectrum
    real, imag = unpack(spectrum)
    mixed_real = jnp.zeros((C, 16), F32)
    mixed_imag = jnp.zeros((C, 16), F32)
    for i in range(C):
        s_real = real[i // 8][i % 8 : i % 8 + 1, :16]
        s_imag = imag[i // 8][i % 8 : i % 8 + 1, :16]
        w_real, w_imag = weights[0, i], weights[1, i]
        mixed_real += w_real * s_real - w_imag * s_imag
        mixed_imag += w_real * s_imag + w_imag * s_real
    tile = pack(mixed_real, mixed_imag) * (mode_weight() * (1.0 / GRID))
    all_gather(tile, comm)
    expand(comm[6], up[...], rows_out)


def backward_kernel(parts, weights, up_hbm, rows_out, cot_out, *scratch):
    up, load_sem, *comm = scratch
    plane, core, z = place()
    load = pltpu.make_async_copy(up_hbm.at[plane * 2 + core], up, load_sem)
    load.start()
    greet()
    greeted()
    for g in range(GROUPS):
        pair_copy(parts, comm, g).start()
    cot = reduce_scatter(parts, comm) * mode_weight()
    cot_out[...] = cot
    real, imag = unpack(cot)
    y_real = jnp.concatenate([tile[:, :16] for tile in real], axis=0)
    y_imag = jnp.concatenate([tile[:, :16] for tile in imag], axis=0)
    pulled_real, pulled_imag = [], []
    for g in range(GROUPS):
        w_real, w_imag = weights[0, g * 8 : g * 8 + 8], weights[1, g * 8 : g * 8 + 8]
        pulled_real.append(jnp.sum(w_real * y_real[None] + w_imag * y_imag[None], axis=1))
        pulled_imag.append(jnp.sum(w_real * y_imag[None] - w_imag * y_real[None], axis=1))
    tile = pack(jnp.concatenate(pulled_real, axis=0), jnp.concatenate(pulled_imag, axis=0))
    all_gather(tile * (1.0 / GRID), comm)
    load.wait()
    expand(comm[6], up[...], rows_out)


def channel_map(weight, transpose):
    size = C * SLAB
    pick = (
        lax.broadcasted_iota(jnp.int32, (size, C), 0) // SLAB
        == lax.broadcasted_iota(jnp.int32, (size, C), 1)
    ).astype(BF16)
    first = lax.dot_general(
        pick, weight, (((1,), (0 if not transpose else 1,)), ((), ())), preferred_element_type=F32
    ).astype(BF16)
    full = lax.dot_general(first, pick, (((1,), (1,)), ((), ())), preferred_element_type=F32)
    same = (
        lax.broadcasted_iota(jnp.int32, (size, size), 0) % SLAB
        == lax.broadcasted_iota(jnp.int32, (size, size), 1) % SLAB
    )
    return jnp.where(same, full, 0.0).astype(BF16)


def point_kernel(
    state, cotangent, rows, weight, bias, basis_hbm, basis_t_hbm, down_hbm,
    slope, seed, parts,
    basis, basis_t, down, mixer, pre, back, sems,
):
    step = pl.program_id(0)
    plane, core, z = place()

    @pl.when(step == 0)
    def _():
        loads = [
            pltpu.make_async_copy(basis_hbm.at[z], basis, sems.at[0]),
            pltpu.make_async_copy(basis_t_hbm.at[z], basis_t, sems.at[1]),
            pltpu.make_async_copy(down_hbm.at[plane * 2 + core], down, sems.at[2]),
        ]
        for load in loads:
            load.start()
        mixer[...] = channel_map(weight[...], True)
        for load in loads:
            load.wait()

    size = C * SLAB
    pre[...] = (
        dot(mixer[...], state[...].reshape(size, COLS))
        + dot(rows[...].reshape(size, 256), basis_t[...])
    ).reshape(C, SLAB, COLS)

    def channel(c, carry):
        value = pre[c] + bias[c]
        cdf = 0.5 * (1.0 + lax.erf(value * (1.0 / math.sqrt(2.0))))
        density = jnp.exp(-0.5 * value * value) * (1.0 / math.sqrt(2.0 * math.pi))
        slope[c] = (value * cdf).astype(BF16)
        seed[c] = (cotangent[c].astype(F32) * (cdf + value * density)).astype(BF16)
        return carry

    lax.fori_loop(0, C, channel, 0)
    back[:, pl.ds(pl.multiple_of(step * SLAB, SLAB), SLAB), :] = dot(
        seed[...].reshape(size, COLS), basis[...]
    ).reshape(C, SLAB, 256)

    @pl.when(step == ROWS // SLAB - 1)
    def _():
        for c in range(C):

            def store(value, g=c // 8, row=c % 8):
                parts[g, 0, pl.ds(row, 32, stride=8), :] = value[:32]
                parts[g, 1, pl.ds(row, 32, stride=8), :] = value[32:]

            rows_down(back[c], down[...], store)


def final_kernel(
    seed, rows, weight, spectrum, cot, basis_t_hbm, grad, weight_grad, basis_t, mixer, sem
):
    z = lax.axis_index("narrow")

    @pl.when(pl.program_id(0) == 0)
    def _():
        load = pltpu.make_async_copy(basis_t_hbm.at[z], basis_t, sem)
        load.start()
        mixer[...] = channel_map(weight[...], False)
        x_real, x_imag = unpack(spectrum[...])
        y_real, y_imag = unpack(cot[...])
        c_real = jnp.concatenate([tile[:, :16] for tile in y_real], axis=0)
        c_imag = jnp.concatenate([tile[:, :16] for tile in y_imag], axis=0)
        for i in range(C):
            s_real = x_real[i // 8][i % 8 : i % 8 + 1, :16]
            s_imag = x_imag[i // 8][i % 8 : i % 8 + 1, :16]
            weight_grad[0, i] = s_real * c_real + s_imag * c_imag
            weight_grad[1, i] = s_real * c_imag - s_imag * c_real
        load.wait()

    size = C * SLAB
    grad[...] = (
        (
            dot(mixer[...], seed[...].reshape(size, COLS))
            + dot(rows[...].reshape(size, 256), basis_t[...])
        )
        .astype(BF16)
        .reshape(C, SLAB, COLS)
    )


VMEM = pl.BlockSpec(memory_space=pltpu.VMEM)
HBM = pl.BlockSpec(memory_space=pl.ANY)
SMEM = pl.BlockSpec(memory_space=pltpu.SMEM)


def slab_spec(width):
    return pl.BlockSpec((C, SLAB, width), lambda i: (0, i, 0))


def whole_spec(*shape):
    return pl.BlockSpec(shape, lambda i: (0,) * len(shape))


def params(megabytes, **more):
    return pltpu.CompilerParams(vmem_limit_bytes=megabytes * 1024 * 1024, **more)


def solution(mesh):
    basis_np, basis_t_np = column_tables()
    down_np, up_np = row_tables()

    def per_device(section_state, cotangent, bypass_weight, bias, spectral_weight):
        basis_all, basis_t_all = jnp.asarray(basis_np), jnp.asarray(basis_t_np)
        down_all, up_all = jnp.asarray(down_np), jnp.asarray(up_np)
        tile = jax.ShapeDtypeStruct((8, 128), F32)
        rows_shape = jax.ShapeDtypeStruct((C, ROWS, 256), BF16)
        field = jax.ShapeDtypeStruct((C, ROWS, COLS), BF16)
        parts_shape = jax.ShapeDtypeStruct((GROUPS, 2, 256, 128), F32)

        rows, spectrum = pl.pallas_call(
            forward_kernel,
            out_shape=(rows_shape, tile),
            in_specs=[HBM, VMEM, HBM, HBM, HBM],
            out_specs=(VMEM, VMEM),
            scratch_shapes=[
                pltpu.VMEM((C, ROWS, COLS), BF16),
                pltpu.VMEM((COLS, 256), BF16),
                pltpu.VMEM((128, 256), BF16),
                pltpu.VMEM((256, 192), BF16),
                pltpu.VMEM((GROUPS, 2, 256, 128), F32),
                pltpu.SemaphoreType.DMA((3 + GROUPS,)),
                *COMM_SCRATCH,
            ],
            compiler_params=params(32, collective_id=0, has_side_effects=True),
            name="forward_modes",
        )(section_state, spectral_weight, basis_all, down_all, up_all)

        slope, seed, parts = pl.pallas_call(
            point_kernel,
            grid=(ROWS // SLAB,),
            out_shape=(field, field, parts_shape),
            in_specs=[
                slab_spec(COLS),
                slab_spec(COLS),
                slab_spec(256),
                whole_spec(C, C),
                SMEM,
                HBM,
                HBM,
                HBM,
            ],
            out_specs=(slab_spec(COLS), slab_spec(COLS), whole_spec(GROUPS, 2, 256, 128)),
            scratch_shapes=[
                pltpu.VMEM((COLS, 256), BF16),
                pltpu.VMEM((256, COLS), BF16),
                pltpu.VMEM((128, 256), BF16),
                pltpu.VMEM((C * SLAB, C * SLAB), BF16),
                pltpu.VMEM((C, SLAB, COLS), F32),
                pltpu.VMEM((C, ROWS, 256), F32),
                pltpu.SemaphoreType.DMA((3,)),
            ],
            compiler_params=params(32),
            name="pointwise",
        )(
            section_state, cotangent, rows, bypass_weight, bias,
            basis_all, basis_t_all, down_all,
        )

        back_rows, cot = pl.pallas_call(
            backward_kernel,
            out_shape=(rows_shape, tile),
            in_specs=[VMEM, VMEM, HBM],
            out_specs=(VMEM, VMEM),
            scratch_shapes=[
                pltpu.VMEM((256, 192), BF16),
                pltpu.SemaphoreType.DMA,
                *COMM_SCRATCH,
            ],
            compiler_params=params(32, collective_id=1, has_side_effects=True),
            name="backward_modes",
        )(parts, spectral_weight, up_all)

        state_grad, weight_grad = pl.pallas_call(
            final_kernel,
            grid=(ROWS // SLAB,),
            out_shape=(field, jax.ShapeDtypeStruct((2, C, C, 16), F32)),
            in_specs=[
                slab_spec(COLS),
                slab_spec(256),
                whole_spec(C, C),
                whole_spec(8, 128),
                whole_spec(8, 128),
                HBM,
            ],
            out_specs=(slab_spec(COLS), whole_spec(2, C, C, 16)),
            scratch_shapes=[
                pltpu.VMEM((256, COLS), BF16),
                pltpu.VMEM((C * SLAB, C * SLAB), BF16),
                pltpu.SemaphoreType.DMA,
            ],
            compiler_params=params(32),
            name="state_gradient",
        )(seed, back_rows, bypass_weight, spectrum, cot, basis_t_all)
        return slope, state_grad, weight_grad

    split_modes = P(None, None, None, ("wide", "narrow"))
    tiles = P(None, "wide", "narrow")
    return jax.shard_map(
        per_device,
        mesh=mesh,
        in_specs=(tiles, tiles, P(), P(), split_modes),
        out_specs=(tiles, tiles, split_modes),
        check_vma=False,
    )
```

```python
import math

import jax
import jax.numpy as jnp
import ml_dtypes
import numpy as np
from jax import lax
from jax.experimental import pallas as pl
from jax.experimental.pallas import tpu as pltpu
from jax.sharding import PartitionSpec as P

GRID = 4096
C = 24
MX = 64
MY = 64
WIDE = 32
NARROW = 8
PLANE = 16
ROWS = GRID // WIDE
COLS = GRID // NARROW
GROUPS = C // 8
SLAB = 16
MESH = pl.DeviceIdType.MESH
F32 = jnp.float32
BF16 = jnp.bfloat16


def split_np(values):
    high = values.astype(ml_dtypes.bfloat16)
    low = (values - high.astype(np.float64)).astype(ml_dtypes.bfloat16)
    return high, low


def column_tables():
    m = np.arange(MY)
    phase = (m[None, :] * np.arange(GRID)[:, None]) % GRID * (2.0 * math.pi / GRID)
    cos_y = np.cos(phase).astype(np.float32).reshape(GRID, 4, 1, 16)
    sin_y = np.sin(phase).astype(np.float32).reshape(GRID, 4, 1, 16)
    with_cos = np.concatenate([cos_y, -sin_y], axis=2).reshape(GRID, 128)
    with_sin = np.concatenate([-sin_y, -cos_y], axis=2).reshape(GRID, 128)
    basis = np.concatenate([with_cos, with_sin], axis=1).astype(ml_dtypes.bfloat16)
    basis = basis.reshape(NARROW, COLS, 256)
    return basis, np.ascontiguousarray(basis.transpose(0, 2, 1))


def row_tables():
    r = np.arange(MX)
    core, plane, low = r // 32, (r // 2) % 16, r % 2
    k = 4 * plane + 2 * core + low
    freq = np.where(k < MX // 2, k, k - MX)
    phase = (freq[:, None] * np.arange(GRID)[None, :]) % GRID * (2.0 * math.pi / GRID)
    cos_x = np.cos(phase).reshape(MX, WIDE, ROWS).transpose(1, 0, 2)
    sin_x = np.sin(phase).reshape(MX, WIDE, ROWS).transpose(1, 0, 2)
    both = np.concatenate([cos_x, sin_x], axis=2)
    high, low = split_np(both)
    down = np.concatenate([high, low], axis=1).astype(np.float64) / GRID
    down = down.astype(ml_dtypes.bfloat16)
    high_t, low_t = high.transpose(0, 2, 1), low.transpose(0, 2, 1)
    up = np.ascontiguousarray(np.concatenate([high_t, high_t, low_t], axis=2))
    return down, up


def split(values):
    high = values.astype(BF16)
    return high, (values - high.astype(F32)).astype(BF16)


def dot(a, b):
    return jnp.dot(a, b, preferred_element_type=F32)


def rows_down(part, down, store):
    stacked = jnp.concatenate([part[:, :128], part[:, 128:]], axis=0)
    high, low = split(stacked)
    four = dot(down, jnp.concatenate([high, low], axis=1))
    store(four[:64, :128] + (four[:64, 128:] + four[64:, :128]))


def lanes():
    return lax.broadcasted_iota(jnp.int32, (8, 128), 1)


def roll(tile, shift):
    return pltpu.roll(tile, shift % 128, 1)


def place():
    wide = lax.axis_index("wide")
    z = lax.axis_index("narrow")
    return lax.div(wide, 2), lax.rem(wide, 2), z


def greet():
    plane, core, z = place()
    barrier = pltpu.get_barrier_semaphore()

    def to_plane(d, carry):
        t = lax.rem(plane + d, PLANE)
        pl.semaphore_signal(barrier, inc=1, device_id=(t * 2 + core, z), device_id_type=MESH)
        return carry

    def to_ring(d, carry):
        t = lax.rem(z + d, NARROW)
        pl.semaphore_signal(
            barrier, inc=1, device_id=(plane * 2 + core, t), device_id_type=MESH
        )
        return carry

    pl.semaphore_signal(
        barrier, inc=1, device_id=(plane * 2 + 1 - core, z), device_id_type=MESH
    )
    lax.fori_loop(1, PLANE, to_plane, 0)
    lax.fori_loop(1, NARROW, to_ring, 0)


def greeted():
    pl.semaphore_wait(pltpu.get_barrier_semaphore(), 1 + (PLANE - 1) + (NARROW - 1))


def remote(src, dst, send, recv, wide, z):
    return pltpu.make_async_remote_copy(
        src_ref=src,
        dst_ref=dst,
        send_sem=send,
        recv_sem=recv,
        device_id=(wide, z),
        device_id_type=MESH,
    )


COMM_SCRATCH = [
    pltpu.VMEM((GROUPS, 256, 128), F32),
    pltpu.VMEM((GROUPS, PLANE, 16, 128), F32),
    pltpu.VMEM((NARROW, 8, 128), F32),
    pltpu.VMEM((NARROW, 8, 128), F32),
    pltpu.VMEM((8, 128), F32),
    pltpu.VMEM((NARROW, 8, 128), F32),
    pltpu.VMEM((MX * C, 128), F32),
    pltpu.SemaphoreType.DMA((2, GROUPS)),
    pltpu.SemaphoreType.DMA((1 + GROUPS,)),
    pltpu.SemaphoreType.DMA((2,)),
    pltpu.SemaphoreType.DMA((2,)),
    pltpu.SemaphoreType.DMA((1 + PLANE,)),
    pltpu.SemaphoreType.DMA((2,)),
]
PAIR, SLOTS, PACKED, RING, OWN, FINAL, MODES = range(7)
PAIR_SEM, PLANE_SEM, RING_SEM, GATHER_RING, GATHER_PLANE, GATHER_PAIR = range(7, 13)


def pair_copy(parts, comm, g):
    plane, core, z = place()
    sems = comm[PAIR_SEM]
    return remote(
        parts.at[g, 1 - core],
        comm[PAIR].at[g],
        sems.at[0, g],
        sems.at[1, g],
        plane * 2 + 1 - core,
        z,
    )


def arrived(ref, sem):
    pltpu.make_async_copy(ref, ref, sem).wait()


def ring_sends(copy, z):
    for d in (4, 3, 5, 2, 6, 1, 7):
        copy(lax.rem(z + d, NARROW)).start()


def plane_order():
    steps = [(dy, dx) for dy in range(4) for dx in range(4) if dy or dx]
    hops = (0, 1, 2, 1)
    return sorted(steps, key=lambda step: -hops[step[0]] - hops[step[1]])


def plane_targets(plane):
    y, x = lax.div(plane, 4), lax.rem(plane, 4)
    return [lax.rem(y + dy, 4) * 4 + lax.rem(x + dx, 4) for dy, dx in plane_order()]


def reduce_scatter(parts, comm, meanwhile=None):
    pair, slots, packed, ring = comm[PAIR], comm[SLOTS], comm[PACKED], comm[RING]
    plane_sems, ring_sems = comm[PLANE_SEM], comm[RING_SEM]
    plane, core, z = place()
    targets = plane_targets(plane)

    for g in range(GROUPS):
        pair_copy(parts, comm, g).wait_recv()
        pair[g] = pair[g] + parts[g, core]
        for t in targets:
            remote(
                pair.at[g, pl.ds(pl.multiple_of(t * 16, 16), 16)],
                slots.at[g, plane],
                plane_sems.at[0],
                plane_sems.at[1 + g],
                t * 2 + core,
                z,
            ).start()
        slots[g, plane] = pair[g, pl.ds(pl.multiple_of(plane * 16, 16), 16)]

    if meanwhile is not None:
        meanwhile()

    sums = []
    for g in range(GROUPS):
        arrived(slots.at[g, pl.ds(0, PLANE - 1)], plane_sems.at[1 + g])
        sums.append(jnp.sum(slots[g], axis=0))

    lane_group = lanes() // 32
    for low in range(2):
        for quarter in range(4):
            tile = jnp.zeros((8, 128), F32)
            for g in range(GROUPS):
                moved = roll(sums[g][low * 8 : low * 8 + 8], 32 * (g - quarter))
                tile = jnp.where(lane_group == g, moved, tile)
            packed[low * 4 + quarter] = tile

    def ring_copy(t):
        return remote(
            packed.at[t], ring.at[z], ring_sems.at[0], ring_sems.at[1], plane * 2 + core, t
        )

    ring_sends(ring_copy, z)
    ring[z] = packed[z]
    arrived(ring.at[pl.ds(0, NARROW - 1)], ring_sems.at[1])
    return jnp.sum(ring[...], axis=0)


def reduce_scatter_sent(parts, comm):
    for g in range(GROUPS):
        pair_copy(parts, comm, g).wait_send()
    for g in range(GROUPS):
        arrived(comm[SLOTS].at[g, pl.ds(0, PLANE - 1)], comm[PLANE_SEM].at[0])
    arrived(comm[RING].at[pl.ds(0, NARROW - 1)], comm[RING_SEM].at[0])


def pack(real, imag):
    pad = jnp.zeros((8, 96), F32)
    lane_group = lanes() // 32
    tile = jnp.zeros((8, 128), F32)
    for g in range(GROUPS):
        rows = slice(g * 8, g * 8 + 8)
        wide_tile = jnp.concatenate([real[rows], imag[rows], pad], axis=1)
        tile = jnp.where(lane_group == g, roll(wide_tile, 32 * g), tile)
    return tile


def all_gather(tile, comm, meanwhile=None):
    own, ring, modes = comm[OWN], comm[FINAL], comm[MODES]
    ring_sems, plane_sems, pair_sems = comm[GATHER_RING], comm[GATHER_PLANE], comm[GATHER_PAIR]
    plane, core, z = place()
    own[...] = tile

    def ring_copy(t):
        return remote(own, ring.at[z], ring_sems.at[0], ring_sems.at[1], plane * 2 + core, t)

    ring_sends(ring_copy, z)
    ring[z] = tile
    arrived(ring.at[pl.ds(0, NARROW - 1)], ring_sems.at[1])

    def chunk(which, j):
        return modes.at[pl.ds(pl.multiple_of((which * PLANE + j) * 48, 48), 48)]

    lane_group = lanes() // 32
    blocks = []
    for low in range(2):
        for g in range(GROUPS):
            block = jnp.zeros((8, 128), F32)
            for quarter in range(4):
                moved = roll(ring[low * 4 + quarter], 32 * (quarter - g))
                block = jnp.where(lane_group == quarter, moved, block)
            blocks.append(block)
    modes[pl.ds(pl.multiple_of((core * PLANE + plane) * 48, 48), 48)] = jnp.concatenate(
        blocks, axis=0
    )

    def plane_copy(t, j):
        return remote(
            chunk(core, j), chunk(core, j), plane_sems.at[0], plane_sems.at[1 + j], t * 2 + core, z
        )

    def pair_forward(j):
        return remote(
            chunk(core, j),
            chunk(core, j),
            pair_sems.at[0],
            pair_sems.at[1],
            plane * 2 + 1 - core,
            z,
        )

    targets = plane_targets(plane)
    for t in targets:
        plane_copy(t, plane).start()
    pair_forward(plane).start()
    if meanwhile is not None:
        meanwhile()
    for j in reversed(targets):
        plane_copy(plane, j).wait_recv()
        pair_forward(j).start()
    other = modes.at[pl.ds(pl.multiple_of((1 - core) * PLANE * 48, 48), PLANE * 48)]
    arrived(other, pair_sems.at[1])
    arrived(other, pair_sems.at[0])
    arrived(modes.at[pl.ds(0, (PLANE - 1) * 48)], plane_sems.at[0])
    arrived(ring.at[pl.ds(0, NARROW - 1)], ring_sems.at[0])


def expand(modes, up, out_ref):
    for c in range(0, C, 2):
        both = jnp.concatenate(
            [modes[pl.ds(c + i, MX, stride=C), :] for i in range(2)], axis=1
        )
        high, low = split(both)
        rows = dot(up, jnp.concatenate([high, low, high], axis=0))
        for i in range(2):
            at = slice(i * 128, i * 128 + 128)
            out_ref[c + i] = jnp.concatenate([rows[:128, at], rows[128:, at]], axis=1).astype(
                BF16
            )


def unpack(tile):
    real = [roll(tile, -32 * g) for g in range(GROUPS)]
    imag = [roll(tile, -32 * g - 16) for g in range(GROUPS)]
    return real, imag


def mode_weight():
    z = lax.axis_index("narrow")
    first = jnp.logical_and(lanes() % 16 == 0, lax.rem(z, 4) == 0)
    return jnp.where(first, 1.0, 2.0).astype(F32)


def channel_map(weight, transpose):
    size = C * SLAB
    pick = (
        lax.broadcasted_iota(jnp.int32, (size, C), 0) // SLAB
        == lax.broadcasted_iota(jnp.int32, (size, C), 1)
    ).astype(BF16)
    first = lax.dot_general(
        pick, weight, (((1,), (0 if not transpose else 1,)), ((), ())), preferred_element_type=F32
    ).astype(BF16)
    full = lax.dot_general(first, pick, (((1,), (1,)), ((), ())), preferred_element_type=F32)
    same = (
        lax.broadcasted_iota(jnp.int32, (size, size), 0) % SLAB
        == lax.broadcasted_iota(jnp.int32, (size, size), 1) % SLAB
    )
    return jnp.where(same, full, 0.0).astype(BF16)


def slab(s):
    return pl.ds(pl.multiple_of(s * SLAB, SLAB), SLAB)


def mix(weights, spectrum):
    real, imag = unpack(spectrum)
    mixed_real = jnp.zeros((C, 16), F32)
    mixed_imag = jnp.zeros((C, 16), F32)
    for i in range(C):
        s_real = real[i // 8][i % 8 : i % 8 + 1, :16]
        s_imag = imag[i // 8][i % 8 : i % 8 + 1, :16]
        w_real, w_imag = weights[0, i], weights[1, i]
        mixed_real += w_real * s_real - w_imag * s_imag
        mixed_imag += w_real * s_imag + w_imag * s_real
    return pack(mixed_real, mixed_imag)


def columns(tile):
    real, imag = unpack(tile)
    return (
        jnp.concatenate([part[:, :16] for part in real], axis=0),
        jnp.concatenate([part[:, :16] for part in imag], axis=0),
    )


def mix_back(weights, cot):
    y_real, y_imag = columns(cot)
    pulled_real, pulled_imag = [], []
    for g in range(GROUPS):
        w_real, w_imag = weights[0, g * 8 : g * 8 + 8], weights[1, g * 8 : g * 8 + 8]
        pulled_real.append(jnp.sum(w_real * y_real[None] + w_imag * y_imag[None], axis=1))
        pulled_imag.append(jnp.sum(w_real * y_imag[None] - w_imag * y_real[None], axis=1))
    return pack(jnp.concatenate(pulled_real, axis=0), jnp.concatenate(pulled_imag, axis=0))


def weight_terms(spectrum, cot, weight_grad):
    x_real, x_imag = unpack(spectrum)
    c_real, c_imag = columns(cot)
    for i in range(C):
        s_real = x_real[i // 8][i % 8 : i % 8 + 1, :16]
        s_imag = x_imag[i // 8][i % 8 : i % 8 + 1, :16]
        weight_grad[0, i] = s_real * c_real + s_imag * c_imag
        weight_grad[1, i] = s_real * c_imag - s_imag * c_real


def map_channels(mixer, source, target):
    size = C * SLAB

    def step(s, carry):
        value = dot(mixer[...], source[:, slab(s), :].reshape(size, COLS))
        target[:, slab(s), :] = value.reshape(C, SLAB, COLS)
        return carry

    lax.fori_loop(0, ROWS // SLAB, step, 0)


def main_kernel(
    state_hbm, cotangent_hbm, weight, bias, weights, basis_hbm, basis_t_hbm, down_hbm, up_hbm,
    slope, linear, back_rows, weight_grad,
    state, cotangent, seed, rows, back, basis, basis_t, down, up, mixer, mixer_t,
    parts, back_parts, load_sems, *comms,
):
    comm, back_comm = comms[: len(COMM_SCRATCH)], comms[len(COMM_SCRATCH) :]
    plane, core, z = place()
    wide = plane * 2 + core
    size = C * SLAB
    loads = [
        pltpu.make_async_copy(basis_hbm.at[z], basis, load_sems.at[0]),
        pltpu.make_async_copy(down_hbm.at[wide], down, load_sems.at[1]),
    ]
    for g in range(GROUPS):
        at = pl.ds(g * 8, 8)
        loads.append(pltpu.make_async_copy(state_hbm.at[at], state.at[at], load_sems.at[2 + g]))
    loads += [
        pltpu.make_async_copy(up_hbm.at[wide], up, load_sems.at[5]),
        pltpu.make_async_copy(basis_t_hbm.at[z], basis_t, load_sems.at[6]),
        pltpu.make_async_copy(cotangent_hbm, cotangent, load_sems.at[7]),
    ]
    for load in loads:
        load.start()
    greet()
    for load in loads[:2]:
        load.wait()

    def send_parts(source, to, peers, g):
        for row in range(8):

            def store(value, row=row):
                to[g, 0, pl.ds(row, 32, stride=8), :] = value[:32]
                to[g, 1, pl.ds(row, 32, stride=8), :] = value[32:]

            rows_down(source(g * 8 + row), down[...], store)
        if g == 0 and peers is comm:
            greeted()
        pair_copy(to, peers, g).start()

    for g in range(GROUPS):
        loads[2 + g].wait()
        send_parts(lambda c: dot(state[c], basis[...]), parts, comm, g)

    def bypass():
        mixer[...] = channel_map(weight[...], False)
        mixer_t[...] = channel_map(weight[...], True)
        map_channels(mixer_t, state, linear)

    spectrum = reduce_scatter(parts, comm, bypass)
    tile = mix(weights, spectrum) * (mode_weight() * (1.0 / GRID))
    for load in loads[5:]:
        load.wait()
    all_gather(tile, comm, lambda: reduce_scatter_sent(parts, comm))
    expand(comm[MODES], up[...], rows)

    def point(s, carry):
        linear[:, slab(s), :] += dot(
            rows[:, slab(s), :].reshape(size, 256), basis_t[...]
        ).reshape(C, SLAB, COLS)

        def channel(c, carry):
            value = linear[c, slab(s), :] + bias[c]
            cdf = 0.5 * (1.0 + lax.erf(value * (1.0 / math.sqrt(2.0))))
            density = jnp.exp(-0.5 * value * value) * (1.0 / math.sqrt(2.0 * math.pi))
            slope[c, slab(s), :] = (value * cdf).astype(BF16)
            seed[c, slab(s), :] = (
                cotangent[c, slab(s), :].astype(F32) * (cdf + value * density)
            ).astype(BF16)
            return carry

        lax.fori_loop(0, C, channel, 0)
        back[:, slab(s), :] = dot(seed[:, slab(s), :].reshape(size, COLS), basis[...]).reshape(
            C, SLAB, 256
        )
        return carry

    lax.fori_loop(0, ROWS // SLAB, point, 0)
    for g in range(GROUPS):
        send_parts(lambda c: back[c], back_parts, back_comm, g)
    cot = reduce_scatter(
        back_parts, back_comm, lambda: map_channels(mixer, seed, linear)
    ) * mode_weight()

    def meanwhile():
        weight_terms(spectrum, cot, weight_grad)
        reduce_scatter_sent(back_parts, back_comm)

    all_gather(mix_back(weights, cot) * (1.0 / GRID), back_comm, meanwhile)
    expand(back_comm[MODES], up[...], back_rows)


def final_kernel(
    slope, linear, rows, basis_t_hbm, slope_out, grad_out, basis_t, grad, sems, slope_sem, load_sem
):
    z = lax.axis_index("narrow")
    slope_copy = pltpu.make_async_copy(slope, slope_out, slope_sem)
    slope_copy.start()
    load = pltpu.make_async_copy(basis_t_hbm.at[z], basis_t, load_sem)
    load.start()
    load.wait()
    size = C * SLAB
    copies = []
    for s in range(ROWS // SLAB):
        at = pl.ds(s * SLAB, SLAB)
        value = linear[:, at, :].reshape(size, COLS) + dot(
            rows[:, at, :].reshape(size, 256), basis_t[...]
        )
        grad[:, at, :] = value.astype(BF16).reshape(C, SLAB, COLS)
        copy = pltpu.make_async_copy(grad.at[:, at, :], grad_out.at[:, at, :], sems.at[s])
        copy.start()
        copies.append(copy)
    for copy in copies:
        copy.wait()
    slope_copy.wait()


VMEM = pl.BlockSpec(memory_space=pltpu.VMEM)
HBM = pl.BlockSpec(memory_space=pltpu.HBM)
SMEM = pl.BlockSpec(memory_space=pltpu.SMEM)


def params(megabytes, **more):
    return pltpu.CompilerParams(vmem_limit_bytes=megabytes * 1024 * 1024, **more)


def solution(mesh):
    basis_np, basis_t_np = column_tables()
    down_np, up_np = row_tables()

    def per_device(section_state, cotangent, bypass_weight, bias, spectral_weight):
        basis_all, basis_t_all, down_all, up_all, section_state, cotangent = (
            pltpu.with_memory_space_constraint(jnp.asarray(array), pltpu.HBM)
            for array in (basis_np, basis_t_np, down_np, up_np, section_state, cotangent)
        )
        rows_shape = jax.ShapeDtypeStruct((C, ROWS, 256), BF16)
        field = jax.ShapeDtypeStruct((C, ROWS, COLS), BF16)
        wide_field = jax.ShapeDtypeStruct((C, ROWS, COLS), F32)

        slope, linear, rows, weight_grad = pl.pallas_call(
            main_kernel,
            out_shape=(field, wide_field, rows_shape, jax.ShapeDtypeStruct((2, C, C, 16), F32)),
            in_specs=[HBM, HBM, VMEM, SMEM, VMEM, HBM, HBM, HBM, HBM],
            out_specs=(VMEM, VMEM, VMEM, VMEM),
            scratch_shapes=[
                pltpu.VMEM((C, ROWS, COLS), BF16),
                pltpu.VMEM((C, ROWS, COLS), BF16),
                pltpu.VMEM((C, ROWS, COLS), BF16),
                pltpu.VMEM((C, ROWS, 256), BF16),
                pltpu.VMEM((C, ROWS, 256), F32),
                pltpu.VMEM((COLS, 256), BF16),
                pltpu.VMEM((256, COLS), BF16),
                pltpu.VMEM((128, 256), BF16),
                pltpu.VMEM((256, 192), BF16),
                pltpu.VMEM((C * SLAB, C * SLAB), BF16),
                pltpu.VMEM((C * SLAB, C * SLAB), BF16),
                pltpu.VMEM((GROUPS, 2, 256, 128), F32),
                pltpu.VMEM((GROUPS, 2, 256, 128), F32),
                pltpu.SemaphoreType.DMA((8,)),
                *COMM_SCRATCH,
                *COMM_SCRATCH,
            ],
            compiler_params=params(26, collective_id=0, has_side_effects=True),
            name="section",
        )(
            section_state, cotangent, bypass_weight, bias, spectral_weight,
            basis_all, basis_t_all, down_all, up_all,
        )

        slope, state_grad = pl.pallas_call(
            final_kernel,
            out_shape=(field, field),
            in_specs=[VMEM, VMEM, VMEM, HBM],
            out_specs=(HBM, HBM),
            scratch_shapes=[
                pltpu.VMEM((256, COLS), BF16),
                pltpu.VMEM((C, ROWS, COLS), BF16),
                pltpu.SemaphoreType.DMA((ROWS // SLAB,)),
                pltpu.SemaphoreType.DMA,
                pltpu.SemaphoreType.DMA,
            ],
            compiler_params=params(16),
            name="state_gradient",
        )(slope, linear, rows, basis_t_all)
        return slope, state_grad, weight_grad

    split_modes = P(None, None, None, ("wide", "narrow"))
    tiles = P(None, "wide", "narrow")
    return jax.shard_map(
        per_device,
        mesh=mesh,
        in_specs=(tiles, tiles, P(), P(), split_modes),
        out_specs=(tiles, tiles, split_modes),
        check_vma=False,
    )
```

```python
import math

import jax
import jax.numpy as jnp
import ml_dtypes
import numpy as np
from jax import lax
from jax.experimental import pallas as pl
from jax.experimental.pallas import tpu as pltpu
from jax.sharding import PartitionSpec as P

GRID = 4096
C = 24
MX = 64
MY = 64
WIDE = 32
NARROW = 8
PLANE = 16
ROWS = GRID // WIDE
COLS = GRID // NARROW
GROUPS = C // 8
SLAB = 16
MESH = pl.DeviceIdType.MESH
F32 = jnp.float32
BF16 = jnp.bfloat16


def split_np(values):
    high = values.astype(ml_dtypes.bfloat16)
    low = (values - high.astype(np.float64)).astype(ml_dtypes.bfloat16)
    return high, low


def column_tables():
    m = np.arange(MY)
    phase = (m[None, :] * np.arange(GRID)[:, None]) % GRID * (2.0 * math.pi / GRID)
    cos_y = np.cos(phase).astype(np.float32).reshape(GRID, 4, 1, 16)
    sin_y = np.sin(phase).astype(np.float32).reshape(GRID, 4, 1, 16)
    with_cos = np.concatenate([cos_y, -sin_y], axis=2).reshape(GRID, 128)
    with_sin = np.concatenate([-sin_y, -cos_y], axis=2).reshape(GRID, 128)
    basis = np.concatenate([with_cos, with_sin], axis=1).astype(ml_dtypes.bfloat16)
    basis = basis.reshape(NARROW, COLS, 256)
    return basis, np.ascontiguousarray(basis.transpose(0, 2, 1))


def row_tables():
    r = np.arange(MX)
    core, plane, low = r // 32, (r // 2) % 16, r % 2
    k = 4 * plane + 2 * core + low
    freq = np.where(k < MX // 2, k, k - MX)
    phase = (freq[:, None] * np.arange(GRID)[None, :]) % GRID * (2.0 * math.pi / GRID)
    cos_x = np.cos(phase).reshape(MX, WIDE, ROWS).transpose(1, 0, 2)
    sin_x = np.sin(phase).reshape(MX, WIDE, ROWS).transpose(1, 0, 2)
    both = np.concatenate([cos_x, sin_x], axis=2)
    high, low = split_np(both)
    down = np.concatenate([high, low], axis=1).astype(np.float64) / GRID
    down = down.astype(ml_dtypes.bfloat16)
    high_t, low_t = high.transpose(0, 2, 1), low.transpose(0, 2, 1)
    up = np.ascontiguousarray(np.concatenate([high_t, high_t, low_t], axis=2))
    return down, up


def split(values):
    high = values.astype(BF16)
    return high, (values - high.astype(F32)).astype(BF16)


def dot(a, b):
    return jnp.dot(a, b, preferred_element_type=F32)


def rows_down(part, down, store):
    stacked = jnp.concatenate([part[:, :128], part[:, 128:]], axis=0)
    high, low = split(stacked)
    four = dot(down, jnp.concatenate([high, low], axis=1))
    store(four[:64, :128] + (four[:64, 128:] + four[64:, :128]))


def lanes():
    return lax.broadcasted_iota(jnp.int32, (8, 128), 1)


def roll(tile, shift):
    return pltpu.roll(tile, shift % 128, 1)


def place():
    wide = lax.axis_index("wide")
    z = lax.axis_index("narrow")
    return lax.div(wide, 2), lax.rem(wide, 2), z


def greet():
    plane, core, z = place()
    barrier = pltpu.get_barrier_semaphore()

    def to_plane(d, carry):
        t = lax.rem(plane + d, PLANE)
        pl.semaphore_signal(barrier, inc=1, device_id=(t * 2 + core, z), device_id_type=MESH)
        return carry

    def to_ring(d, carry):
        t = lax.rem(z + d, NARROW)
        pl.semaphore_signal(
            barrier, inc=1, device_id=(plane * 2 + core, t), device_id_type=MESH
        )
        return carry

    pl.semaphore_signal(
        barrier, inc=1, device_id=(plane * 2 + 1 - core, z), device_id_type=MESH
    )
    lax.fori_loop(1, PLANE, to_plane, 0)
    lax.fori_loop(1, NARROW, to_ring, 0)


def greeted():
    pl.semaphore_wait(pltpu.get_barrier_semaphore(), 1 + (PLANE - 1) + (NARROW - 1))


def remote(src, dst, send, recv, wide, z):
    return pltpu.make_async_remote_copy(
        src_ref=src,
        dst_ref=dst,
        send_sem=send,
        recv_sem=recv,
        device_id=(wide, z),
        device_id_type=MESH,
    )


COMM_SCRATCH = [
    pltpu.VMEM((GROUPS, 256, 128), F32),
    pltpu.VMEM((GROUPS, PLANE, 16, 128), F32),
    pltpu.VMEM((NARROW, 8, 128), F32),
    pltpu.VMEM((NARROW, 8, 128), F32),
    pltpu.VMEM((8, 128), F32),
    pltpu.VMEM((NARROW, 8, 128), F32),
    pltpu.VMEM((GROUPS, MX * 8, 128), F32),
    pltpu.SemaphoreType.DMA((2, GROUPS)),
    pltpu.SemaphoreType.DMA((1 + GROUPS,)),
    pltpu.SemaphoreType.DMA((2,)),
    pltpu.SemaphoreType.DMA((2,)),
    pltpu.SemaphoreType.DMA((1 + GROUPS * PLANE,)),
    pltpu.SemaphoreType.DMA((1 + GROUPS,)),
]
PAIR, SLOTS, PACKED, RING, OWN, FINAL, MODES = range(7)
PAIR_SEM, PLANE_SEM, RING_SEM, GATHER_RING, GATHER_PLANE, GATHER_PAIR = range(7, 13)


def pair_copy(parts, comm, g):
    plane, core, z = place()
    sems = comm[PAIR_SEM]
    return remote(
        parts.at[g, 1 - core],
        comm[PAIR].at[g],
        sems.at[0, g],
        sems.at[1, g],
        plane * 2 + 1 - core,
        z,
    )


def arrived(ref, sem):
    pltpu.make_async_copy(ref, ref, sem).wait()


def ring_sends(copy, z):
    for d in (4, 3, 5, 2, 6, 1, 7):
        copy(lax.rem(z + d, NARROW)).start()


def plane_order():
    steps = [(dy, dx) for dy in range(4) for dx in range(4) if dy or dx]
    hops = (0, 1, 2, 1)
    return sorted(steps, key=lambda step: -hops[step[0]] - hops[step[1]])


def plane_targets(plane):
    y, x = lax.div(plane, 4), lax.rem(plane, 4)
    return [lax.rem(y + dy, 4) * 4 + lax.rem(x + dx, 4) for dy, dx in plane_order()]


def plane_stage(parts, comm, g):
    pair, slots, plane_sems = comm[PAIR], comm[SLOTS], comm[PLANE_SEM]
    plane, core, z = place()
    pair_copy(parts, comm, g).wait_recv()
    pair[g] = pair[g] + parts[g, core]
    for t in plane_targets(plane):
        remote(
            pair.at[g, pl.ds(pl.multiple_of(t * 16, 16), 16)],
            slots.at[g, plane],
            plane_sems.at[0],
            plane_sems.at[1 + g],
            t * 2 + core,
            z,
        ).start()
    slots[g, plane] = pair[g, pl.ds(pl.multiple_of(plane * 16, 16), 16)]


def reduce_scatter(comm):
    slots, packed, ring = comm[SLOTS], comm[PACKED], comm[RING]
    plane_sems, ring_sems = comm[PLANE_SEM], comm[RING_SEM]
    plane, core, z = place()

    sums = []
    for g in range(GROUPS):
        arrived(slots.at[g, pl.ds(0, PLANE - 1)], plane_sems.at[1 + g])
        sums.append(jnp.sum(slots[g], axis=0))

    lane_group = lanes() // 32
    for low in range(2):
        for quarter in range(4):
            tile = jnp.zeros((8, 128), F32)
            for g in range(GROUPS):
                moved = roll(sums[g][low * 8 : low * 8 + 8], 32 * (g - quarter))
                tile = jnp.where(lane_group == g, moved, tile)
            packed[low * 4 + quarter] = tile

    def ring_copy(t):
        return remote(
            packed.at[t], ring.at[z], ring_sems.at[0], ring_sems.at[1], plane * 2 + core, t
        )

    ring_sends(ring_copy, z)
    ring[z] = packed[z]
    arrived(ring.at[pl.ds(0, NARROW - 1)], ring_sems.at[1])
    return jnp.sum(ring[...], axis=0)


def reduce_scatter_sent(parts, comm):
    for g in range(GROUPS):
        pair_copy(parts, comm, g).wait_send()
    for g in range(GROUPS):
        arrived(comm[SLOTS].at[g, pl.ds(0, PLANE - 1)], comm[PLANE_SEM].at[0])
    arrived(comm[RING].at[pl.ds(0, NARROW - 1)], comm[RING_SEM].at[0])


def pack(real, imag):
    pad = jnp.zeros((8, 96), F32)
    lane_group = lanes() // 32
    tile = jnp.zeros((8, 128), F32)
    for g in range(GROUPS):
        rows = slice(g * 8, g * 8 + 8)
        wide_tile = jnp.concatenate([real[rows], imag[rows], pad], axis=1)
        tile = jnp.where(lane_group == g, roll(wide_tile, 32 * g), tile)
    return tile


def all_gather(tile, comm, meanwhile, consume):
    own, ring, modes = comm[OWN], comm[FINAL], comm[MODES]
    ring_sems, plane_sems, pair_sems = comm[GATHER_RING], comm[GATHER_PLANE], comm[GATHER_PAIR]
    plane, core, z = place()
    own[...] = tile

    def ring_copy(t):
        return remote(own, ring.at[z], ring_sems.at[0], ring_sems.at[1], plane * 2 + core, t)

    ring_sends(ring_copy, z)
    ring[z] = tile
    arrived(ring.at[pl.ds(0, NARROW - 1)], ring_sems.at[1])

    def chunk(g, which, j):
        return modes.at[g, pl.ds(pl.multiple_of((which * PLANE + j) * 16, 16), 16)]

    def plane_copy(g, t, j):
        return remote(
            chunk(g, core, j),
            chunk(g, core, j),
            plane_sems.at[0],
            plane_sems.at[1 + g * PLANE + j],
            t * 2 + core,
            z,
        )

    def pair_forward(g, j):
        return remote(
            chunk(g, core, j),
            chunk(g, core, j),
            pair_sems.at[0],
            pair_sems.at[1 + g],
            plane * 2 + 1 - core,
            z,
        )

    targets = plane_targets(plane)
    lane_group = lanes() // 32
    for g in range(GROUPS):
        blocks = []
        for low in range(2):
            block = jnp.zeros((8, 128), F32)
            for quarter in range(4):
                moved = roll(ring[low * 4 + quarter], 32 * (quarter - g))
                block = jnp.where(lane_group == quarter, moved, block)
            blocks.append(block)
        modes[g, pl.ds(pl.multiple_of((core * PLANE + plane) * 16, 16), 16)] = jnp.concatenate(
            blocks, axis=0
        )
        for t in targets:
            plane_copy(g, t, plane).start()
        pair_forward(g, plane).start()
    meanwhile()

    def forward(g):
        for j in reversed(targets):
            plane_copy(g, plane, j).wait_recv()
            pair_forward(g, j).start()

    def other(g):
        return modes.at[g, pl.ds(pl.multiple_of((1 - core) * PLANE * 16, 16), PLANE * 16)]

    forward(0)
    for g in range(GROUPS):
        if g + 1 < GROUPS:
            forward(g + 1)
        arrived(other(g), pair_sems.at[1 + g])
        consume(g)


def all_gather_sent(comm):
    modes = comm[MODES]
    for g in range(GROUPS):
        arrived(modes.at[g, pl.ds(0, PLANE * 16)], comm[GATHER_PAIR].at[0])
        arrived(modes.at[g, pl.ds(0, (PLANE - 1) * 16)], comm[GATHER_PLANE].at[0])
    arrived(comm[FINAL].at[pl.ds(0, NARROW - 1)], comm[GATHER_RING].at[0])


def expand(modes, up, g, out_ref):
    for row in range(0, 8, 2):
        both = jnp.concatenate(
            [modes[g, pl.ds(row + i, MX, stride=8), :] for i in range(2)], axis=1
        )
        high, low = split(both)
        rows = dot(up, jnp.concatenate([high, low, high], axis=0))
        for i in range(2):
            at = slice(i * 128, i * 128 + 128)
            out_ref[g * 8 + row + i] = jnp.concatenate(
                [rows[:128, at], rows[128:, at]], axis=1
            ).astype(BF16)


def unpack(tile):
    real = [roll(tile, -32 * g) for g in range(GROUPS)]
    imag = [roll(tile, -32 * g - 16) for g in range(GROUPS)]
    return real, imag


def mode_weight():
    z = lax.axis_index("narrow")
    first = jnp.logical_and(lanes() % 16 == 0, lax.rem(z, 4) == 0)
    return jnp.where(first, 1.0, 2.0).astype(F32)


def channel_map(weight, transpose):
    size = C * SLAB
    pick = (
        lax.broadcasted_iota(jnp.int32, (size, C), 0) // SLAB
        == lax.broadcasted_iota(jnp.int32, (size, C), 1)
    ).astype(BF16)
    first = lax.dot_general(
        pick, weight, (((1,), (0 if not transpose else 1,)), ((), ())), preferred_element_type=F32
    ).astype(BF16)
    full = lax.dot_general(first, pick, (((1,), (1,)), ((), ())), preferred_element_type=F32)
    same = (
        lax.broadcasted_iota(jnp.int32, (size, size), 0) % SLAB
        == lax.broadcasted_iota(jnp.int32, (size, size), 1) % SLAB
    )
    return jnp.where(same, full, 0.0).astype(BF16)


def slab(s):
    return pl.ds(pl.multiple_of(s * SLAB, SLAB), SLAB)


def mix(weights, spectrum):
    real, imag = unpack(spectrum)
    mixed_real = jnp.zeros((C, 16), F32)
    mixed_imag = jnp.zeros((C, 16), F32)
    for i in range(C):
        s_real = real[i // 8][i % 8 : i % 8 + 1, :16]
        s_imag = imag[i // 8][i % 8 : i % 8 + 1, :16]
        w_real, w_imag = weights[0, i], weights[1, i]
        mixed_real += w_real * s_real - w_imag * s_imag
        mixed_imag += w_real * s_imag + w_imag * s_real
    return pack(mixed_real, mixed_imag)


def columns(tile):
    real, imag = unpack(tile)
    return (
        jnp.concatenate([part[:, :16] for part in real], axis=0),
        jnp.concatenate([part[:, :16] for part in imag], axis=0),
    )


def mix_back(weights, cot):
    y_real, y_imag = columns(cot)
    pulled_real, pulled_imag = [], []
    for g in range(GROUPS):
        w_real, w_imag = weights[0, g * 8 : g * 8 + 8], weights[1, g * 8 : g * 8 + 8]
        pulled_real.append(jnp.sum(w_real * y_real[None] + w_imag * y_imag[None], axis=1))
        pulled_imag.append(jnp.sum(w_real * y_imag[None] - w_imag * y_real[None], axis=1))
    return pack(jnp.concatenate(pulled_real, axis=0), jnp.concatenate(pulled_imag, axis=0))


def weight_terms(spectrum, cot, weight_grad):
    x_real, x_imag = unpack(spectrum)
    c_real, c_imag = columns(cot)
    for i in range(C):
        s_real = x_real[i // 8][i % 8 : i % 8 + 1, :16]
        s_imag = x_imag[i // 8][i % 8 : i % 8 + 1, :16]
        weight_grad[0, i] = (s_real * c_real + s_imag * c_imag).T
        weight_grad[1, i] = (s_real * c_imag - s_imag * c_real).T


def map_channels(mixer, source, target):
    size = C * SLAB

    def step(s, carry):
        value = dot(mixer[...], source[:, slab(s), :].reshape(size, COLS))
        target[:, slab(s), :] = value.reshape(C, SLAB, COLS)
        return carry

    lax.fori_loop(0, ROWS // SLAB, step, 0)


def main_kernel(
    state_hbm, cotangent_hbm, weight_hbm, bias_hbm, weights_hbm,
    basis_hbm, basis_t_hbm, down_hbm, up_hbm,
    slope, linear, back_rows, weight_grad,
    state, cotangent, seed, rows, back, weight, bias, weights_t, weights,
    basis, basis_t, down, up, mixer, mixer_t,
    parts, back_parts, load_sems, *comms,
):
    comm, back_comm = comms[: len(COMM_SCRATCH)], comms[len(COMM_SCRATCH) :]
    plane, core, z = place()
    wide = plane * 2 + core
    loads = [
        pltpu.make_async_copy(basis_hbm.at[z], basis, load_sems.at[0]),
        pltpu.make_async_copy(down_hbm.at[wide], down, load_sems.at[1]),
    ]
    for g in range(GROUPS):
        at = pl.ds(g * 8, 8)
        loads.append(pltpu.make_async_copy(state_hbm.at[at], state.at[at], load_sems.at[2 + g]))
    loads += [
        pltpu.make_async_copy(weight_hbm, weight, load_sems.at[5]),
        pltpu.make_async_copy(weights_hbm, weights_t, load_sems.at[6]),
        pltpu.make_async_copy(up_hbm.at[wide], up, load_sems.at[7]),
        pltpu.make_async_copy(basis_t_hbm.at[z], basis_t, load_sems.at[8]),
        pltpu.make_async_copy(bias_hbm, bias, load_sems.at[9]),
        pltpu.make_async_copy(cotangent_hbm, cotangent, load_sems.at[10]),
    ]
    for load in loads:
        load.start()
    greet()
    for load in loads[:2]:
        load.wait()

    def send_parts(to, peers, g):
        for row in range(8):

            def store(value, row=row):
                to[g, 0, pl.ds(row, 32, stride=8), :] = value[:32]
                to[g, 1, pl.ds(row, 32, stride=8), :] = value[32:]

            rows_down(back[g * 8 + row], down[...], store)
        if g == 0 and peers is comm:
            greeted()
        pair_copy(to, peers, g).start()
        if g:
            plane_stage(to, peers, g - 1)

    def to_columns(source, g):
        at = slice(g * 8, g * 8 + 8)
        back[at] = dot(source[at].reshape(8 * ROWS, COLS), basis[...]).reshape(8, ROWS, 256)

    for g in range(GROUPS):
        loads[2 + g].wait()
        to_columns(state, g)
        send_parts(parts, comm, g)
    plane_stage(parts, comm, GROUPS - 1)

    for load in loads[5:]:
        load.wait()
    mixer_t[...] = channel_map(weight[...], True)
    map_channels(mixer_t, state, linear)
    for i in range(C):
        weights[0, i] = weights_t[0, i].T
        weights[1, i] = weights_t[1, i].T
    mixer[...] = channel_map(weight[...], False)

    spectrum = reduce_scatter(comm)
    tile = mix(weights, spectrum) * (mode_weight() * (1.0 / GRID))

    def point(g):
        expand(comm[MODES], up[...], g, rows)
        at = slice(g * 8, g * 8 + 8)
        linear[at] = linear[at] + dot(
            rows[at].reshape(8 * ROWS, 256), basis_t[...]
        ).reshape(8, ROWS, COLS)
        for c in range(g * 8, g * 8 + 8):
            for s in range(ROWS // SLAB):
                x = slice(s * SLAB, s * SLAB + SLAB)
                value = linear[c, x] + bias[c]
                cdf = 0.5 + 0.5 * lax.erf(value * (1.0 / math.sqrt(2.0)))
                density = jnp.exp(-0.5 * value * value) * (1.0 / math.sqrt(2.0 * math.pi))
                slope[c, x] = (value * cdf).astype(BF16)
                seed[c, x] = (cotangent[c, x].astype(F32) * (cdf + value * density)).astype(BF16)
        to_columns(seed, g)
        send_parts(back_parts, back_comm, g)

    all_gather(tile, comm, lambda: reduce_scatter_sent(parts, comm), point)
    plane_stage(back_parts, back_comm, GROUPS - 1)
    map_channels(mixer, seed, linear)
    cot = reduce_scatter(back_comm) * mode_weight()

    def meanwhile():
        weight_terms(spectrum, cot, weight_grad)
        reduce_scatter_sent(back_parts, back_comm)
        all_gather_sent(comm)

    all_gather(
        mix_back(weights, cot) * (1.0 / GRID),
        back_comm,
        meanwhile,
        lambda g: expand(back_comm[MODES], up[...], g, back_rows),
    )
    all_gather_sent(back_comm)


def final_kernel(
    slope, weight_grad, linear, rows, basis_t_hbm,
    slope_out, weight_grad_out, grad_out,
    basis_t, grad, sems, done_sems, load_sem,
):
    z = lax.axis_index("narrow")
    done = [
        pltpu.make_async_copy(slope, slope_out, done_sems.at[0]),
        pltpu.make_async_copy(weight_grad, weight_grad_out, done_sems.at[1]),
    ]
    for copy in done:
        copy.start()
    load = pltpu.make_async_copy(basis_t_hbm.at[z], basis_t, load_sem)
    load.start()
    load.wait()
    size = C * SLAB
    copies = []
    for s in range(ROWS // SLAB):
        at = pl.ds(s * SLAB, SLAB)
        value = linear[:, at, :].reshape(size, COLS) + dot(
            rows[:, at, :].reshape(size, 256), basis_t[...]
        )
        grad[:, at, :] = value.astype(BF16).reshape(C, SLAB, COLS)
        copy = pltpu.make_async_copy(grad.at[:, at, :], grad_out.at[:, at, :], sems.at[s])
        copy.start()
        copies.append(copy)
    for copy in copies + done:
        copy.wait()


VMEM = pl.BlockSpec(memory_space=pltpu.VMEM)
HBM = pl.BlockSpec(memory_space=pltpu.HBM)
SMEM = pl.BlockSpec(memory_space=pltpu.SMEM)


def params(megabytes, **more):
    return pltpu.CompilerParams(vmem_limit_bytes=megabytes * 1024 * 1024, **more)


def solution(mesh):
    basis_np, basis_t_np = column_tables()
    down_np, up_np = row_tables()

    def per_device(section_state, cotangent, bypass_weight, bias, spectral_weight):
        def in_hbm(array):
            return pltpu.with_memory_space_constraint(jnp.asarray(array), pltpu.HBM)

        basis_t_all = in_hbm(basis_t_np)
        tables = (in_hbm(basis_np), basis_t_all, in_hbm(down_np), in_hbm(up_np))
        arguments = (
            section_state, cotangent, bypass_weight, bias, jnp.swapaxes(spectral_weight, 2, 3)
        )
        rows_shape = jax.ShapeDtypeStruct((C, ROWS, 256), BF16)
        field = jax.ShapeDtypeStruct((C, ROWS, COLS), BF16)
        modes_shape = jax.ShapeDtypeStruct((2, C, 16, C), F32)
        wide_field = jax.ShapeDtypeStruct((C, ROWS, COLS), F32)

        slope, linear, rows, weight_grad = pl.pallas_call(
            main_kernel,
            out_shape=(field, wide_field, rows_shape, modes_shape),
            in_specs=[HBM] * 9,
            out_specs=(VMEM, VMEM, VMEM, VMEM),
            scratch_shapes=[
                pltpu.VMEM((C, ROWS, COLS), BF16),
                pltpu.VMEM((C, ROWS, COLS), BF16),
                pltpu.VMEM((C, ROWS, COLS), BF16),
                pltpu.VMEM((C, ROWS, 256), BF16),
                pltpu.VMEM((C, ROWS, 256), F32),
                pltpu.VMEM((C, C), BF16),
                pltpu.SMEM((C,), F32),
                pltpu.VMEM((2, C, 16, C), F32),
                pltpu.VMEM((2, C, C, 16), F32),
                pltpu.VMEM((COLS, 256), BF16),
                pltpu.VMEM((256, COLS), BF16),
                pltpu.VMEM((128, 256), BF16),
                pltpu.VMEM((256, 192), BF16),
                pltpu.VMEM((C * SLAB, C * SLAB), BF16),
                pltpu.VMEM((C * SLAB, C * SLAB), BF16),
                pltpu.VMEM((GROUPS, 2, 256, 128), F32),
                pltpu.VMEM((GROUPS, 2, 256, 128), F32),
                pltpu.SemaphoreType.DMA((11,)),
                *COMM_SCRATCH,
                *COMM_SCRATCH,
            ],
            compiler_params=params(26, collective_id=0, has_side_effects=True),
            name="section",
        )(*(in_hbm(array) for array in arguments), *tables)

        slope, weight_grad, state_grad = pl.pallas_call(
            final_kernel,
            out_shape=(field, modes_shape, field),
            in_specs=[VMEM, VMEM, VMEM, VMEM, HBM],
            out_specs=(HBM, HBM, HBM),
            scratch_shapes=[
                pltpu.VMEM((256, COLS), BF16),
                pltpu.VMEM((C, ROWS, COLS), BF16),
                pltpu.SemaphoreType.DMA((ROWS // SLAB,)),
                pltpu.SemaphoreType.DMA((2,)),
                pltpu.SemaphoreType.DMA,
            ],
            compiler_params=params(16),
            name="state_gradient",
        )(slope, weight_grad, linear, rows, basis_t_all)
        return slope, state_grad, jnp.swapaxes(weight_grad, 2, 3)

    split_modes = P(None, None, None, ("wide", "narrow"))
    tiles = P(None, "wide", "narrow")
    return jax.shard_map(
        per_device,
        mesh=mesh,
        in_specs=(tiles, tiles, P(), P(), split_modes),
        out_specs=(tiles, tiles, split_modes),
        check_vma=False,
    )
```

```python
import math

import jax
import jax.numpy as jnp
import ml_dtypes
import numpy as np
from jax import lax
from jax.experimental import pallas as pl
from jax.experimental.pallas import tpu as pltpu
from jax.sharding import PartitionSpec as P

GRID = 4096
C = 24
MX = 64
MY = 64
WIDE = 32
NARROW = 8
PLANE = 16
ROWS = GRID // WIDE
COLS = GRID // NARROW
GROUPS = C // 8
SLAB = 16
MESH = pl.DeviceIdType.MESH
F32 = jnp.float32
BF16 = jnp.bfloat16


def split_np(values):
    high = values.astype(ml_dtypes.bfloat16)
    low = (values - high.astype(np.float64)).astype(ml_dtypes.bfloat16)
    return high, low


def column_tables():
    m = np.arange(MY)
    phase = (m[None, :] * np.arange(GRID)[:, None]) % GRID * (2.0 * math.pi / GRID)
    cos_y = np.cos(phase).astype(np.float32).reshape(GRID, 4, 1, 16)
    sin_y = np.sin(phase).astype(np.float32).reshape(GRID, 4, 1, 16)
    with_cos = np.concatenate([cos_y, -sin_y], axis=2).reshape(GRID, 128)
    with_sin = np.concatenate([-sin_y, -cos_y], axis=2).reshape(GRID, 128)
    basis = np.concatenate([with_cos, with_sin], axis=1).astype(ml_dtypes.bfloat16)
    basis = basis.reshape(NARROW, COLS, 256)
    return basis, np.ascontiguousarray(basis.transpose(0, 2, 1))


def row_tables():
    r = np.arange(MX)
    core, plane, low = r // 32, (r // 2) % 16, r % 2
    k = 4 * plane + 2 * core + low
    freq = np.where(k < MX // 2, k, k - MX)
    phase = (freq[:, None] * np.arange(GRID)[None, :]) % GRID * (2.0 * math.pi / GRID)
    cos_x = np.cos(phase).reshape(MX, WIDE, ROWS).transpose(1, 0, 2)
    sin_x = np.sin(phase).reshape(MX, WIDE, ROWS).transpose(1, 0, 2)
    both = np.concatenate([cos_x, sin_x], axis=2)
    high, low = split_np(both)
    down = np.concatenate([high, low], axis=1).astype(np.float64) / GRID
    down = down.astype(ml_dtypes.bfloat16)
    high_t, low_t = high.transpose(0, 2, 1), low.transpose(0, 2, 1)
    up = np.ascontiguousarray(np.concatenate([high_t, high_t, low_t], axis=2))
    return down, up


def split(values):
    high = values.astype(BF16)
    return high, (values - high.astype(F32)).astype(BF16)


def dot(a, b):
    return jnp.dot(a, b, preferred_element_type=F32)


def rows_down(part, down, store):
    stacked = jnp.concatenate([part[:, :128], part[:, 128:]], axis=0)
    high, low = split(stacked)
    four = dot(down, jnp.concatenate([high, low], axis=1))
    store(four[:64, :128] + (four[:64, 128:] + four[64:, :128]))


def lanes():
    return lax.broadcasted_iota(jnp.int32, (8, 128), 1)


def roll(tile, shift):
    return pltpu.roll(tile, shift % 128, 1)


def place():
    wide = lax.axis_index("wide")
    z = lax.axis_index("narrow")
    return lax.div(wide, 2), lax.rem(wide, 2), z


def greet():
    plane, core, z = place()
    barrier = pltpu.get_barrier_semaphore()

    def to_plane(d, carry):
        t = lax.rem(plane + d, PLANE)
        pl.semaphore_signal(barrier, inc=1, device_id=(t * 2 + core, z), device_id_type=MESH)
        return carry

    def to_ring(d, carry):
        t = lax.rem(z + d, NARROW)
        pl.semaphore_signal(
            barrier, inc=1, device_id=(plane * 2 + core, t), device_id_type=MESH
        )
        return carry

    pl.semaphore_signal(
        barrier, inc=1, device_id=(plane * 2 + 1 - core, z), device_id_type=MESH
    )
    lax.fori_loop(1, PLANE, to_plane, 0)
    lax.fori_loop(1, NARROW, to_ring, 0)


def greeted():
    pl.semaphore_wait(pltpu.get_barrier_semaphore(), 1 + (PLANE - 1) + (NARROW - 1))


def remote(src, dst, send, recv, wide, z):
    return pltpu.make_async_remote_copy(
        src_ref=src,
        dst_ref=dst,
        send_sem=send,
        recv_sem=recv,
        device_id=(wide, z),
        device_id_type=MESH,
    )


COMM_SCRATCH = [
    pltpu.VMEM((GROUPS, 256, 128), F32),
    pltpu.VMEM((GROUPS, PLANE, 16, 128), F32),
    pltpu.VMEM((NARROW, 8, 128), F32),
    pltpu.VMEM((NARROW, 8, 128), F32),
    pltpu.VMEM((8, 128), F32),
    pltpu.VMEM((NARROW, 8, 128), F32),
    pltpu.VMEM((GROUPS, MX * 8, 128), F32),
    pltpu.SemaphoreType.DMA((2, GROUPS)),
    pltpu.SemaphoreType.DMA((1 + GROUPS,)),
    pltpu.SemaphoreType.DMA((2,)),
    pltpu.SemaphoreType.DMA((2,)),
    pltpu.SemaphoreType.DMA((1 + GROUPS,)),
    pltpu.SemaphoreType.DMA((1 + GROUPS,)),
]
PAIR, SLOTS, PACKED, RING, OWN, FINAL, MODES = range(7)
PAIR_SEM, PLANE_SEM, RING_SEM, GATHER_RING, GATHER_PLANE, GATHER_PAIR = range(7, 13)


def pair_copy(parts, comm, g):
    plane, core, z = place()
    sems = comm[PAIR_SEM]
    return remote(
        parts.at[g, 1 - core],
        comm[PAIR].at[g],
        sems.at[0, g],
        sems.at[1, g],
        plane * 2 + 1 - core,
        z,
    )


def arrived(ref, sem):
    pltpu.make_async_copy(ref, ref, sem).wait()


def ring_sends(copy, z):
    for d in (4, 3, 5, 2, 6, 1, 7):
        copy(lax.rem(z + d, NARROW)).start()


def plane_order():
    steps = [(dy, dx) for dy in range(4) for dx in range(4) if dy or dx]
    hops = (0, 1, 2, 1)
    return sorted(steps, key=lambda step: -hops[step[0]] - hops[step[1]])


def plane_targets(plane):
    y, x = lax.div(plane, 4), lax.rem(plane, 4)
    return [lax.rem(y + dy, 4) * 4 + lax.rem(x + dx, 4) for dy, dx in plane_order()]


def plane_stage(parts, comm, g):
    pair, slots, plane_sems = comm[PAIR], comm[SLOTS], comm[PLANE_SEM]
    plane, core, z = place()
    pair_copy(parts, comm, g).wait_recv()
    pair[g] = pair[g] + parts[g, core]
    for t in plane_targets(plane):
        remote(
            pair.at[g, pl.ds(pl.multiple_of(t * 16, 16), 16)],
            slots.at[g, plane],
            plane_sems.at[0],
            plane_sems.at[1 + g],
            t * 2 + core,
            z,
        ).start()
    slots[g, plane] = pair[g, pl.ds(pl.multiple_of(plane * 16, 16), 16)]


def reduce_scatter(comm):
    slots, packed, ring = comm[SLOTS], comm[PACKED], comm[RING]
    plane_sems, ring_sems = comm[PLANE_SEM], comm[RING_SEM]
    plane, core, z = place()

    sums = []
    for g in range(GROUPS):
        arrived(slots.at[g, pl.ds(0, PLANE - 1)], plane_sems.at[1 + g])
        sums.append(jnp.sum(slots[g], axis=0))

    lane_group = lanes() // 32
    for low in range(2):
        for quarter in range(4):
            tile = jnp.zeros((8, 128), F32)
            for g in range(GROUPS):
                moved = roll(sums[g][low * 8 : low * 8 + 8], 32 * (g - quarter))
                tile = jnp.where(lane_group == g, moved, tile)
            packed[low * 4 + quarter] = tile

    def ring_copy(t):
        return remote(
            packed.at[t], ring.at[z], ring_sems.at[0], ring_sems.at[1], plane * 2 + core, t
        )

    ring_sends(ring_copy, z)
    ring[z] = packed[z]
    arrived(ring.at[pl.ds(0, NARROW - 1)], ring_sems.at[1])
    return jnp.sum(ring[...], axis=0)


def reduce_scatter_sent(parts, comm):
    for g in range(GROUPS):
        pair_copy(parts, comm, g).wait_send()
    for g in range(GROUPS):
        arrived(comm[SLOTS].at[g, pl.ds(0, PLANE - 1)], comm[PLANE_SEM].at[0])
    arrived(comm[RING].at[pl.ds(0, NARROW - 1)], comm[RING_SEM].at[0])


def pack(real, imag):
    pad = jnp.zeros((8, 96), F32)
    lane_group = lanes() // 32
    tile = jnp.zeros((8, 128), F32)
    for g in range(GROUPS):
        rows = slice(g * 8, g * 8 + 8)
        wide_tile = jnp.concatenate([real[rows], imag[rows], pad], axis=1)
        tile = jnp.where(lane_group == g, roll(wide_tile, 32 * g), tile)
    return tile


def all_gather(tile, comm, meanwhile, consume):
    own, ring, modes = comm[OWN], comm[FINAL], comm[MODES]
    ring_sems, plane_sems, pair_sems = comm[GATHER_RING], comm[GATHER_PLANE], comm[GATHER_PAIR]
    plane, core, z = place()
    own[...] = tile

    def ring_copy(t):
        return remote(own, ring.at[z], ring_sems.at[0], ring_sems.at[1], plane * 2 + core, t)

    ring_sends(ring_copy, z)
    ring[z] = tile
    arrived(ring.at[pl.ds(0, NARROW - 1)], ring_sems.at[1])

    def chunk(g):
        return modes.at[g, pl.ds(pl.multiple_of((core * PLANE + plane) * 16, 16), 16)]

    def plane_copy(g, t):
        return remote(
            chunk(g),
            chunk(g),
            plane_sems.at[0],
            plane_sems.at[1 + g],
            t * 2 + core,
            z,
        )

    def half(g, which):
        return modes.at[g, pl.ds(pl.multiple_of(which * 256, 256), 256)]

    def forward(g):
        arrived(modes.at[g, pl.ds(0, (PLANE - 1) * 16)], plane_sems.at[1 + g])
        remote(
            half(g, core),
            half(g, core),
            pair_sems.at[0],
            pair_sems.at[1 + g],
            plane * 2 + 1 - core,
            z,
        ).start()

    targets = plane_targets(plane)
    lane_group = lanes() // 32
    for g in range(GROUPS):
        blocks = []
        for low in range(2):
            block = jnp.zeros((8, 128), F32)
            for quarter in range(4):
                moved = roll(ring[low * 4 + quarter], 32 * (quarter - g))
                block = jnp.where(lane_group == quarter, moved, block)
            blocks.append(block)
        modes[g, pl.ds(pl.multiple_of((core * PLANE + plane) * 16, 16), 16)] = jnp.concatenate(
            blocks, axis=0
        )
        for t in targets:
            plane_copy(g, t).start()
    meanwhile()

    forward(0)
    for g in range(GROUPS):
        if g + 1 < GROUPS:
            forward(g + 1)
        arrived(half(g, 1 - core), pair_sems.at[1 + g])
        consume(g)


def all_gather_sent(comm):
    modes = comm[MODES]
    for g in range(GROUPS):
        arrived(modes.at[g, pl.ds(0, PLANE * 16)], comm[GATHER_PAIR].at[0])
        arrived(modes.at[g, pl.ds(0, (PLANE - 1) * 16)], comm[GATHER_PLANE].at[0])
    arrived(comm[FINAL].at[pl.ds(0, NARROW - 1)], comm[GATHER_RING].at[0])


def expand(modes, up, g, out_ref):
    for row in range(0, 8, 2):
        both = jnp.concatenate(
            [modes[g, pl.ds(row + i, MX, stride=8), :] for i in range(2)], axis=1
        )
        high, low = split(both)
        rows = dot(up, jnp.concatenate([high, low, high], axis=0))
        for i in range(2):
            at = slice(i * 128, i * 128 + 128)
            out_ref[g * 8 + row + i] = jnp.concatenate(
                [rows[:128, at], rows[128:, at]], axis=1
            ).astype(BF16)


def unpack(tile):
    real = [roll(tile, -32 * g) for g in range(GROUPS)]
    imag = [roll(tile, -32 * g - 16) for g in range(GROUPS)]
    return real, imag


def mode_weight():
    z = lax.axis_index("narrow")
    first = jnp.logical_and(lanes() % 16 == 0, lax.rem(z, 4) == 0)
    return jnp.where(first, 1.0, 2.0).astype(F32)


def channel_map(weight, transpose):
    size = C * SLAB
    pick = (
        lax.broadcasted_iota(jnp.int32, (size, C), 0) // SLAB
        == lax.broadcasted_iota(jnp.int32, (size, C), 1)
    ).astype(BF16)
    first = lax.dot_general(
        pick, weight, (((1,), (0 if not transpose else 1,)), ((), ())), preferred_element_type=F32
    ).astype(BF16)
    full = lax.dot_general(first, pick, (((1,), (1,)), ((), ())), preferred_element_type=F32)
    same = (
        lax.broadcasted_iota(jnp.int32, (size, size), 0) % SLAB
        == lax.broadcasted_iota(jnp.int32, (size, size), 1) % SLAB
    )
    return jnp.where(same, full, 0.0).astype(BF16)


def slab(s):
    return pl.ds(pl.multiple_of(s * SLAB, SLAB), SLAB)


def mix(weights, spectrum):
    real, imag = unpack(spectrum)
    mixed_real = jnp.zeros((C, 16), F32)
    mixed_imag = jnp.zeros((C, 16), F32)
    for i in range(C):
        s_real = real[i // 8][i % 8 : i % 8 + 1, :16]
        s_imag = imag[i // 8][i % 8 : i % 8 + 1, :16]
        w_real, w_imag = weights[0, i], weights[1, i]
        mixed_real += w_real * s_real - w_imag * s_imag
        mixed_imag += w_real * s_imag + w_imag * s_real
    return pack(mixed_real, mixed_imag)


def columns(tile):
    real, imag = unpack(tile)
    return (
        jnp.concatenate([part[:, :16] for part in real], axis=0),
        jnp.concatenate([part[:, :16] for part in imag], axis=0),
    )


def mix_back(weights, cot):
    y_real, y_imag = columns(cot)
    pulled_real, pulled_imag = [], []
    for g in range(GROUPS):
        w_real, w_imag = weights[0, g * 8 : g * 8 + 8], weights[1, g * 8 : g * 8 + 8]
        pulled_real.append(jnp.sum(w_real * y_real[None] + w_imag * y_imag[None], axis=1))
        pulled_imag.append(jnp.sum(w_real * y_imag[None] - w_imag * y_real[None], axis=1))
    return pack(jnp.concatenate(pulled_real, axis=0), jnp.concatenate(pulled_imag, axis=0))


def weight_terms(spectrum, cot, weight_grad):
    x_real, x_imag = unpack(spectrum)
    c_real, c_imag = columns(cot)
    for i in range(C):
        s_real = x_real[i // 8][i % 8 : i % 8 + 1, :16]
        s_imag = x_imag[i // 8][i % 8 : i % 8 + 1, :16]
        weight_grad[0, i] = (s_real * c_real + s_imag * c_imag).T
        weight_grad[1, i] = (s_real * c_imag - s_imag * c_real).T


def map_channels(mixer, source, target):
    size = C * SLAB

    def step(s, carry):
        value = dot(mixer[...], source[:, slab(s), :].reshape(size, COLS))
        target[:, slab(s), :] = value.reshape(C, SLAB, COLS)
        return carry

    lax.fori_loop(0, ROWS // SLAB, step, 0)


def main_kernel(
    state_hbm, cotangent_hbm, weight_hbm, bias_hbm, weights_hbm,
    basis_hbm, basis_t_hbm, down_hbm, up_hbm,
    slope, linear, back_rows, weight_grad, basis_t,
    state, cotangent, seed, rows, back, weight, bias, weights_t, weights,
    basis, down, up, mixer, mixer_t,
    parts, back_parts, load_sems, *comms,
):
    comm, back_comm = comms[: len(COMM_SCRATCH)], comms[len(COMM_SCRATCH) :]
    plane, core, z = place()
    wide = plane * 2 + core
    loads = [
        pltpu.make_async_copy(basis_hbm.at[z], basis, load_sems.at[0]),
        pltpu.make_async_copy(down_hbm.at[wide], down, load_sems.at[1]),
    ]
    for g in range(GROUPS):
        at = pl.ds(g * 8, 8)
        loads.append(pltpu.make_async_copy(state_hbm.at[at], state.at[at], load_sems.at[2 + g]))
    loads += [
        pltpu.make_async_copy(weight_hbm, weight, load_sems.at[5]),
        pltpu.make_async_copy(weights_hbm, weights_t, load_sems.at[6]),
        pltpu.make_async_copy(up_hbm.at[wide], up, load_sems.at[7]),
        pltpu.make_async_copy(basis_t_hbm.at[z], basis_t, load_sems.at[8]),
        pltpu.make_async_copy(bias_hbm, bias, load_sems.at[9]),
        pltpu.make_async_copy(cotangent_hbm, cotangent, load_sems.at[10]),
    ]
    for load in loads[:5]:
        load.start()
    greet()
    for load in loads[:2]:
        load.wait()

    def send_parts(to, peers, g):
        for row in range(8):

            def store(value, row=row):
                to[g, 0, pl.ds(row, 32, stride=8), :] = value[:32]
                to[g, 1, pl.ds(row, 32, stride=8), :] = value[32:]

            rows_down(back[g * 8 + row], down[...], store)
        if g == 0 and peers is comm:
            greeted()
        pair_copy(to, peers, g).start()
        if g:
            plane_stage(to, peers, g - 1)

    def to_columns(source, g):
        at = slice(g * 8, g * 8 + 8)
        back[at] = dot(source[at].reshape(8 * ROWS, COLS), basis[...]).reshape(8, ROWS, 256)

    for g in range(GROUPS):
        loads[2 + g].wait()
        if g == GROUPS - 1:
            for load in loads[5:]:
                load.start()
        to_columns(state, g)
        send_parts(parts, comm, g)
    plane_stage(parts, comm, GROUPS - 1)

    loads[5].wait()
    mixer_t[...] = channel_map(weight[...], True)
    map_channels(mixer_t, state, linear)
    for load in loads[6:]:
        load.wait()
    for i in range(C):
        weights[0, i] = weights_t[0, i].T
        weights[1, i] = weights_t[1, i].T
    mixer[...] = channel_map(weight[...], False)

    spectrum = reduce_scatter(comm)
    tile = mix(weights, spectrum) * (mode_weight() * (1.0 / GRID))

    def point(g):
        expand(comm[MODES], up[...], g, rows)
        at = slice(g * 8, g * 8 + 8)
        linear[at] = linear[at] + dot(
            rows[at].reshape(8 * ROWS, 256), basis_t[...]
        ).reshape(8, ROWS, COLS)
        for c in range(g * 8, g * 8 + 8):
            for s in range(ROWS // SLAB):
                x = slice(s * SLAB, s * SLAB + SLAB)
                value = linear[c, x] + bias[c]
                cdf = 0.5 + 0.5 * lax.erf(value * (1.0 / math.sqrt(2.0)))
                density = jnp.exp(-0.5 * value * value) * (1.0 / math.sqrt(2.0 * math.pi))
                slope[c, x] = (value * cdf).astype(BF16)
                seed[c, x] = (cotangent[c, x].astype(F32) * (cdf + value * density)).astype(BF16)
        to_columns(seed, g)
        send_parts(back_parts, back_comm, g)

    all_gather(tile, comm, lambda: reduce_scatter_sent(parts, comm), point)
    plane_stage(back_parts, back_comm, GROUPS - 1)
    map_channels(mixer, seed, linear)
    cot = reduce_scatter(back_comm) * mode_weight()

    def meanwhile():
        weight_terms(spectrum, cot, weight_grad)
        reduce_scatter_sent(back_parts, back_comm)
        all_gather_sent(comm)

    all_gather(
        mix_back(weights, cot) * (1.0 / GRID),
        back_comm,
        meanwhile,
        lambda g: expand(back_comm[MODES], up[...], g, back_rows),
    )
    all_gather_sent(back_comm)


def final_kernel(
    slope, weight_grad, linear, rows, basis_t,
    slope_out, weight_grad_out, grad_out,
    grad, sems, done_sems,
):
    done = [
        pltpu.make_async_copy(slope, slope_out, done_sems.at[0]),
        pltpu.make_async_copy(weight_grad, weight_grad_out, done_sems.at[1]),
    ]
    for copy in done:
        copy.start()
    size = C * SLAB
    copies = []
    for s in range(ROWS // SLAB):
        at = pl.ds(s * SLAB, SLAB)
        value = linear[:, at, :].reshape(size, COLS) + dot(
            rows[:, at, :].reshape(size, 256), basis_t[...]
        )
        grad[:, at, :] = value.astype(BF16).reshape(C, SLAB, COLS)
        copy = pltpu.make_async_copy(grad.at[:, at, :], grad_out.at[:, at, :], sems.at[s])
        copy.start()
        copies.append(copy)
    for copy in copies + done:
        copy.wait()


VMEM = pl.BlockSpec(memory_space=pltpu.VMEM)
HBM = pl.BlockSpec(memory_space=pltpu.HBM)
SMEM = pl.BlockSpec(memory_space=pltpu.SMEM)


def params(megabytes, **more):
    return pltpu.CompilerParams(vmem_limit_bytes=megabytes * 1024 * 1024, **more)


def solution(mesh):
    basis_np, basis_t_np = column_tables()
    down_np, up_np = row_tables()

    def per_device(section_state, cotangent, bypass_weight, bias, spectral_weight):
        def in_hbm(array):
            return pltpu.with_memory_space_constraint(jnp.asarray(array), pltpu.HBM)

        tables = [in_hbm(table) for table in (basis_np, basis_t_np, down_np, up_np)]
        arguments = (
            section_state, cotangent, bypass_weight, bias, jnp.swapaxes(spectral_weight, 2, 3)
        )
        rows_shape = jax.ShapeDtypeStruct((C, ROWS, 256), BF16)
        field = jax.ShapeDtypeStruct((C, ROWS, COLS), BF16)
        modes_shape = jax.ShapeDtypeStruct((2, C, 16, C), F32)
        basis_shape = jax.ShapeDtypeStruct((256, COLS), BF16)
        wide_field = jax.ShapeDtypeStruct((C, ROWS, COLS), F32)

        slope, linear, rows, weight_grad, basis_t = pl.pallas_call(
            main_kernel,
            out_shape=(field, wide_field, rows_shape, modes_shape, basis_shape),
            in_specs=[HBM] * 9,
            out_specs=(VMEM,) * 5,
            scratch_shapes=[
                pltpu.VMEM((C, ROWS, COLS), BF16),
                pltpu.VMEM((C, ROWS, COLS), BF16),
                pltpu.VMEM((C, ROWS, COLS), BF16),
                pltpu.VMEM((C, ROWS, 256), BF16),
                pltpu.VMEM((C, ROWS, 256), F32),
                pltpu.VMEM((C, C), BF16),
                pltpu.SMEM((C,), F32),
                pltpu.VMEM((2, C, 16, C), F32),
                pltpu.VMEM((2, C, C, 16), F32),
                pltpu.VMEM((COLS, 256), BF16),
                pltpu.VMEM((128, 256), BF16),
                pltpu.VMEM((256, 192), BF16),
                pltpu.VMEM((C * SLAB, C * SLAB), BF16),
                pltpu.VMEM((C * SLAB, C * SLAB), BF16),
                pltpu.VMEM((GROUPS, 2, 256, 128), F32),
                pltpu.VMEM((GROUPS, 2, 256, 128), F32),
                pltpu.SemaphoreType.DMA((11,)),
                *COMM_SCRATCH,
                *COMM_SCRATCH,
            ],
            compiler_params=params(26, collective_id=0, has_side_effects=True),
            name="section",
        )(*(in_hbm(array) for array in arguments), *tables)

        slope, weight_grad, state_grad = pl.pallas_call(
            final_kernel,
            out_shape=(field, modes_shape, field),
            in_specs=[VMEM] * 5,
            out_specs=(HBM, HBM, HBM),
            scratch_shapes=[
                pltpu.VMEM((C, ROWS, COLS), BF16),
                pltpu.SemaphoreType.DMA((ROWS // SLAB,)),
                pltpu.SemaphoreType.DMA((2,)),
            ],
            compiler_params=params(16),
            name="state_gradient",
        )(slope, weight_grad, linear, rows, basis_t)
        return slope, state_grad, jnp.swapaxes(weight_grad, 2, 3)

    split_modes = P(None, None, None, ("wide", "narrow"))
    tiles = P(None, "wide", "narrow")
    return jax.shard_map(
        per_device,
        mesh=mesh,
        in_specs=(tiles, tiles, P(), P(), split_modes),
        out_specs=(tiles, tiles, split_modes),
        check_vma=False,
    )
```

```python
import math

import jax
import jax.numpy as jnp
import ml_dtypes
import numpy as np
from jax import lax
from jax.experimental import pallas as pl
from jax.experimental.pallas import tpu as pltpu
from jax.sharding import PartitionSpec as P

GRID = 4096
C = 24
MX = 64
MY = 64
WIDE = 32
NARROW = 8
PLANE = 16
ROWS = GRID // WIDE
COLS = GRID // NARROW
GROUPS = C // 8
SLAB = 16
MESH = pl.DeviceIdType.MESH
F32 = jnp.float32
BF16 = jnp.bfloat16


def split_np(values):
    high = values.astype(ml_dtypes.bfloat16)
    low = (values - high.astype(np.float64)).astype(ml_dtypes.bfloat16)
    return high, low


def column_tables():
    m = np.arange(MY)
    phase = (m[None, :] * np.arange(GRID)[:, None]) % GRID * (2.0 * math.pi / GRID)
    cos_y = np.cos(phase).astype(np.float32).reshape(GRID, 4, 1, 16)
    sin_y = np.sin(phase).astype(np.float32).reshape(GRID, 4, 1, 16)
    with_cos = np.concatenate([cos_y, -sin_y], axis=2).reshape(GRID, 128)
    with_sin = np.concatenate([-sin_y, -cos_y], axis=2).reshape(GRID, 128)
    basis = np.concatenate([with_cos, with_sin], axis=1).astype(ml_dtypes.bfloat16)
    basis = basis.reshape(NARROW, COLS, 256)
    return basis, np.ascontiguousarray(basis.transpose(0, 2, 1))


def row_tables():
    r = np.arange(MX)
    core, plane, low = r // 32, (r // 2) % 16, r % 2
    k = 4 * plane + 2 * core + low
    freq = np.where(k < MX // 2, k, k - MX)
    phase = (freq[:, None] * np.arange(GRID)[None, :]) % GRID * (2.0 * math.pi / GRID)
    cos_x = np.cos(phase).reshape(MX, WIDE, ROWS).transpose(1, 0, 2)
    sin_x = np.sin(phase).reshape(MX, WIDE, ROWS).transpose(1, 0, 2)
    both = np.concatenate([cos_x, sin_x], axis=2)
    high, low = split_np(both)
    down = np.concatenate([high, low], axis=1).astype(np.float64) / GRID
    down = down.astype(ml_dtypes.bfloat16)
    high_t, low_t = high.transpose(0, 2, 1), low.transpose(0, 2, 1)
    up = np.ascontiguousarray(np.concatenate([high_t, high_t, low_t], axis=2))
    return down, up


def split(values):
    high = values.astype(BF16)
    return high, (values - high.astype(F32)).astype(BF16)


def dot(a, b):
    return jnp.dot(a, b, preferred_element_type=F32)


def rows_down(part, down, store):
    stacked = jnp.concatenate([part[:, :128], part[:, 128:]], axis=0)
    high, low = split(stacked)
    four = dot(down, jnp.concatenate([high, low], axis=1))
    store(four[:64, :128] + (four[:64, 128:] + four[64:, :128]))


def lanes():
    return lax.broadcasted_iota(jnp.int32, (8, 128), 1)


def roll(tile, shift):
    return pltpu.roll(tile, shift % 128, 1)


def place():
    wide = lax.axis_index("wide")
    z = lax.axis_index("narrow")
    return lax.div(wide, 2), lax.rem(wide, 2), z


def greet():
    plane, core, z = place()
    barrier = pltpu.get_barrier_semaphore()

    def to_plane(d, carry):
        t = lax.rem(plane + d, PLANE)
        pl.semaphore_signal(barrier, inc=1, device_id=(t * 2 + core, z), device_id_type=MESH)
        return carry

    def to_ring(d, carry):
        t = lax.rem(z + d, NARROW)
        pl.semaphore_signal(
            barrier, inc=1, device_id=(plane * 2 + core, t), device_id_type=MESH
        )
        return carry

    pl.semaphore_signal(
        barrier, inc=1, device_id=(plane * 2 + 1 - core, z), device_id_type=MESH
    )
    lax.fori_loop(1, PLANE, to_plane, 0)
    lax.fori_loop(1, NARROW, to_ring, 0)


def greeted():
    pl.semaphore_wait(pltpu.get_barrier_semaphore(), 1 + (PLANE - 1) + (NARROW - 1))


def remote(src, dst, send, recv, wide, z):
    return pltpu.make_async_remote_copy(
        src_ref=src,
        dst_ref=dst,
        send_sem=send,
        recv_sem=recv,
        device_id=(wide, z),
        device_id_type=MESH,
    )


COMM_SCRATCH = [
    pltpu.VMEM((GROUPS, 256, 128), F32),
    pltpu.VMEM((GROUPS, PLANE, 16, 128), F32),
    pltpu.VMEM((NARROW, 8, 128), F32),
    pltpu.VMEM((NARROW, 8, 128), F32),
    pltpu.VMEM((8, 128), F32),
    pltpu.VMEM((NARROW, 8, 128), F32),
    pltpu.VMEM((GROUPS, MX * 8, 128), F32),
    pltpu.SemaphoreType.DMA((2, GROUPS)),
    pltpu.SemaphoreType.DMA((1 + GROUPS,)),
    pltpu.SemaphoreType.DMA((2,)),
    pltpu.SemaphoreType.DMA((2,)),
    pltpu.SemaphoreType.DMA((1 + GROUPS,)),
    pltpu.SemaphoreType.DMA((1 + GROUPS,)),
]
PAIR, SLOTS, PACKED, RING, OWN, FINAL, MODES = range(7)
PAIR_SEM, PLANE_SEM, RING_SEM, GATHER_RING, GATHER_PLANE, GATHER_PAIR = range(7, 13)


def pair_copy(parts, comm, g):
    plane, core, z = place()
    sems = comm[PAIR_SEM]
    return remote(
        parts.at[g, 1 - core],
        comm[PAIR].at[g],
        sems.at[0, g],
        sems.at[1, g],
        plane * 2 + 1 - core,
        z,
    )


def arrived(ref, sem):
    pltpu.make_async_copy(ref, ref, sem).wait()


def ring_sends(copy, z):
    for d in (4, 3, 5, 2, 6, 1, 7):
        copy(lax.rem(z + d, NARROW)).start()


def plane_order():
    steps = [(dy, dx) for dy in range(4) for dx in range(4) if dy or dx]
    hops = (0, 1, 2, 1)
    return sorted(steps, key=lambda step: -hops[step[0]] - hops[step[1]])


def plane_targets(plane):
    y, x = lax.div(plane, 4), lax.rem(plane, 4)
    return [lax.rem(y + dy, 4) * 4 + lax.rem(x + dx, 4) for dy, dx in plane_order()]


def plane_stage(parts, comm, g):
    pair, slots, plane_sems = comm[PAIR], comm[SLOTS], comm[PLANE_SEM]
    plane, core, z = place()
    pair_copy(parts, comm, g).wait_recv()
    pair[g] = pair[g] + parts[g, core]
    for t in plane_targets(plane):
        remote(
            pair.at[g, pl.ds(pl.multiple_of(t * 16, 16), 16)],
            slots.at[g, plane],
            plane_sems.at[0],
            plane_sems.at[1 + g],
            t * 2 + core,
            z,
        ).start()
    slots[g, plane] = pair[g, pl.ds(pl.multiple_of(plane * 16, 16), 16)]


def reduce_scatter(comm):
    slots, packed, ring = comm[SLOTS], comm[PACKED], comm[RING]
    plane_sems, ring_sems = comm[PLANE_SEM], comm[RING_SEM]
    plane, core, z = place()

    sums = []
    for g in range(GROUPS):
        arrived(slots.at[g, pl.ds(0, PLANE - 1)], plane_sems.at[1 + g])
        sums.append(jnp.sum(slots[g], axis=0))

    lane_group = lanes() // 32
    for low in range(2):
        for quarter in range(4):
            tile = jnp.zeros((8, 128), F32)
            for g in range(GROUPS):
                moved = roll(sums[g][low * 8 : low * 8 + 8], 32 * (g - quarter))
                tile = jnp.where(lane_group == g, moved, tile)
            packed[low * 4 + quarter] = tile

    def ring_copy(t):
        return remote(
            packed.at[t], ring.at[z], ring_sems.at[0], ring_sems.at[1], plane * 2 + core, t
        )

    ring_sends(ring_copy, z)
    ring[z] = packed[z]
    arrived(ring.at[pl.ds(0, NARROW - 1)], ring_sems.at[1])
    return jnp.sum(ring[...], axis=0)


def reduce_scatter_sent(parts, comm):
    for g in range(GROUPS):
        pair_copy(parts, comm, g).wait_send()
    for g in range(GROUPS):
        arrived(comm[SLOTS].at[g, pl.ds(0, PLANE - 1)], comm[PLANE_SEM].at[0])
    arrived(comm[RING].at[pl.ds(0, NARROW - 1)], comm[RING_SEM].at[0])


def pack(real, imag):
    pad = jnp.zeros((8, 96), F32)
    lane_group = lanes() // 32
    tile = jnp.zeros((8, 128), F32)
    for g in range(GROUPS):
        rows = slice(g * 8, g * 8 + 8)
        wide_tile = jnp.concatenate([real[rows], imag[rows], pad], axis=1)
        tile = jnp.where(lane_group == g, roll(wide_tile, 32 * g), tile)
    return tile


def all_gather(tile, comm, meanwhile, consume, finish=None):
    own, ring, modes = comm[OWN], comm[FINAL], comm[MODES]
    ring_sems, plane_sems, pair_sems = comm[GATHER_RING], comm[GATHER_PLANE], comm[GATHER_PAIR]
    plane, core, z = place()
    own[...] = tile

    def ring_copy(t):
        return remote(own, ring.at[z], ring_sems.at[0], ring_sems.at[1], plane * 2 + core, t)

    ring_sends(ring_copy, z)
    ring[z] = tile
    arrived(ring.at[pl.ds(0, NARROW - 1)], ring_sems.at[1])

    def chunk(g):
        return modes.at[g, pl.ds(pl.multiple_of((core * PLANE + plane) * 16, 16), 16)]

    def plane_copy(g, t):
        return remote(
            chunk(g),
            chunk(g),
            plane_sems.at[0],
            plane_sems.at[1 + g],
            t * 2 + core,
            z,
        )

    def half(g, which):
        return modes.at[g, pl.ds(pl.multiple_of(which * 256, 256), 256)]

    def forward(g):
        arrived(modes.at[g, pl.ds(0, (PLANE - 1) * 16)], plane_sems.at[1 + g])
        remote(
            half(g, core),
            half(g, core),
            pair_sems.at[0],
            pair_sems.at[1 + g],
            plane * 2 + 1 - core,
            z,
        ).start()

    targets = plane_targets(plane)
    lane_group = lanes() // 32
    for g in range(GROUPS):
        blocks = []
        for low in range(2):
            block = jnp.zeros((8, 128), F32)
            for quarter in range(4):
                moved = roll(ring[low * 4 + quarter], 32 * (quarter - g))
                block = jnp.where(lane_group == quarter, moved, block)
            blocks.append(block)
        modes[g, pl.ds(pl.multiple_of((core * PLANE + plane) * 16, 16), 16)] = jnp.concatenate(
            blocks, axis=0
        )
        for t in targets:
            plane_copy(g, t).start()
    meanwhile()

    for g in range(GROUPS):
        forward(g)
    for g in range(GROUPS):
        arrived(half(g, 1 - core), pair_sems.at[1 + g])
        consume(g)
        if g and finish is not None:
            finish(g - 1)
    if finish is not None:
        finish(GROUPS - 1)


def all_gather_sent(comm):
    modes = comm[MODES]
    for g in range(GROUPS):
        arrived(modes.at[g, pl.ds(0, PLANE * 16)], comm[GATHER_PAIR].at[0])
        arrived(modes.at[g, pl.ds(0, (PLANE - 1) * 16)], comm[GATHER_PLANE].at[0])
    arrived(comm[FINAL].at[pl.ds(0, NARROW - 1)], comm[GATHER_RING].at[0])


def expand(modes, up, g, out_ref):
    for row in range(0, 8, 2):
        both = jnp.concatenate(
            [modes[g, pl.ds(row + i, MX, stride=8), :] for i in range(2)], axis=1
        )
        high, low = split(both)
        rows = dot(up, jnp.concatenate([high, low, high], axis=0))
        for i in range(2):
            at = slice(i * 128, i * 128 + 128)
            out_ref[g * 8 + row + i] = jnp.concatenate(
                [rows[:128, at], rows[128:, at]], axis=1
            ).astype(BF16)


def unpack(tile):
    real = [roll(tile, -32 * g) for g in range(GROUPS)]
    imag = [roll(tile, -32 * g - 16) for g in range(GROUPS)]
    return real, imag


def mode_weight():
    z = lax.axis_index("narrow")
    first = jnp.logical_and(lanes() % 16 == 0, lax.rem(z, 4) == 0)
    return jnp.where(first, 1.0, 2.0).astype(F32)


def channel_map(weight, transpose):
    size = C * SLAB
    pick = (
        lax.broadcasted_iota(jnp.int32, (size, C), 0) // SLAB
        == lax.broadcasted_iota(jnp.int32, (size, C), 1)
    ).astype(BF16)
    first = lax.dot_general(
        pick, weight, (((1,), (0 if not transpose else 1,)), ((), ())), preferred_element_type=F32
    ).astype(BF16)
    full = lax.dot_general(first, pick, (((1,), (1,)), ((), ())), preferred_element_type=F32)
    same = (
        lax.broadcasted_iota(jnp.int32, (size, size), 0) % SLAB
        == lax.broadcasted_iota(jnp.int32, (size, size), 1) % SLAB
    )
    return jnp.where(same, full, 0.0).astype(BF16)


def slab(s):
    return pl.ds(pl.multiple_of(s * SLAB, SLAB), SLAB)


def mix(weights, spectrum):
    real, imag = unpack(spectrum)
    mixed_real = jnp.zeros((C, 16), F32)
    mixed_imag = jnp.zeros((C, 16), F32)
    for i in range(C):
        s_real = real[i // 8][i % 8 : i % 8 + 1, :16]
        s_imag = imag[i // 8][i % 8 : i % 8 + 1, :16]
        w_real, w_imag = weights[0, i], weights[1, i]
        mixed_real += w_real * s_real - w_imag * s_imag
        mixed_imag += w_real * s_imag + w_imag * s_real
    return pack(mixed_real, mixed_imag)


def columns(tile):
    real, imag = unpack(tile)
    return (
        jnp.concatenate([part[:, :16] for part in real], axis=0),
        jnp.concatenate([part[:, :16] for part in imag], axis=0),
    )


def mix_back(weights, cot):
    y_real, y_imag = columns(cot)
    pulled_real, pulled_imag = [], []
    for g in range(GROUPS):
        w_real, w_imag = weights[0, g * 8 : g * 8 + 8], weights[1, g * 8 : g * 8 + 8]
        pulled_real.append(jnp.sum(w_real * y_real[None] + w_imag * y_imag[None], axis=1))
        pulled_imag.append(jnp.sum(w_real * y_imag[None] - w_imag * y_real[None], axis=1))
    return pack(jnp.concatenate(pulled_real, axis=0), jnp.concatenate(pulled_imag, axis=0))


def weight_terms(spectrum, cot, weight_grad):
    x_real, x_imag = unpack(spectrum)
    c_real, c_imag = columns(cot)
    for i in range(C):
        s_real = x_real[i // 8][i % 8 : i % 8 + 1, :16]
        s_imag = x_imag[i // 8][i % 8 : i % 8 + 1, :16]
        weight_grad[0, i] = (s_real * c_real + s_imag * c_imag).T
        weight_grad[1, i] = (s_real * c_imag - s_imag * c_real).T


def map_channels(mixer, source, target):
    size = C * SLAB

    def step(s, carry):
        value = dot(mixer[...], source[:, slab(s), :].reshape(size, COLS))
        target[:, slab(s), :] = value.reshape(C, SLAB, COLS)
        return carry

    lax.fori_loop(0, ROWS // SLAB, step, 0)


def main_kernel(
    state_hbm, cotangent_hbm, weight_hbm, bias_hbm, weights_hbm,
    basis_hbm, basis_t_hbm, down_hbm, up_hbm,
    slope, linear, back_rows, weight_grad, basis_t,
    state, cotangent, seed, rows, back, weight, bias, weights_t, weights,
    basis, down, up, mixer, mixer_t,
    parts, back_parts, load_sems, *comms,
):
    comm, back_comm = comms[: len(COMM_SCRATCH)], comms[len(COMM_SCRATCH) :]
    plane, core, z = place()
    wide = plane * 2 + core
    loads = [
        pltpu.make_async_copy(basis_hbm.at[z], basis, load_sems.at[0]),
        pltpu.make_async_copy(down_hbm.at[wide], down, load_sems.at[1]),
    ]
    for g in range(GROUPS):
        at = pl.ds(g * 8, 8)
        loads.append(pltpu.make_async_copy(state_hbm.at[at], state.at[at], load_sems.at[2 + g]))
    loads += [
        pltpu.make_async_copy(weight_hbm, weight, load_sems.at[5]),
        pltpu.make_async_copy(weights_hbm, weights_t, load_sems.at[6]),
        pltpu.make_async_copy(up_hbm.at[wide], up, load_sems.at[7]),
        pltpu.make_async_copy(basis_t_hbm.at[z], basis_t, load_sems.at[8]),
        pltpu.make_async_copy(bias_hbm, bias, load_sems.at[9]),
        pltpu.make_async_copy(cotangent_hbm, cotangent, load_sems.at[10]),
    ]
    for load in loads[:5]:
        load.start()
    greet()
    for load in loads[:2]:
        load.wait()

    def send_parts(to, peers, g):
        for row in range(8):

            def store(value, row=row):
                to[g, 0, pl.ds(row, 32, stride=8), :] = value[:32]
                to[g, 1, pl.ds(row, 32, stride=8), :] = value[32:]

            rows_down(back[g * 8 + row], down[...], store)
        if g == 0 and peers is comm:
            greeted()
        pair_copy(to, peers, g).start()
        if g:
            plane_stage(to, peers, g - 1)

    def to_columns(source, g):
        at = slice(g * 8, g * 8 + 8)
        back[at] = dot(source[at].reshape(8 * ROWS, COLS), basis[...]).reshape(8, ROWS, 256)

    for g in range(GROUPS):
        loads[2 + g].wait()
        if g == GROUPS - 1:
            for load in loads[5:]:
                load.start()
        to_columns(state, g)
        send_parts(parts, comm, g)
    plane_stage(parts, comm, GROUPS - 1)

    loads[5].wait()
    mixer_t[...] = channel_map(weight[...], True)
    map_channels(mixer_t, state, linear)
    for load in loads[6:]:
        load.wait()
    for i in range(C):
        weights[0, i] = weights_t[0, i].T
        weights[1, i] = weights_t[1, i].T
    mixer[...] = channel_map(weight[...], False)

    spectrum = reduce_scatter(comm)
    tile = mix(weights, spectrum) * (mode_weight() * (1.0 / GRID))

    def point(g):
        expand(comm[MODES], up[...], g, rows)
        at = slice(g * 8, g * 8 + 8)
        linear[at] = linear[at] + dot(
            rows[at].reshape(8 * ROWS, 256), basis_t[...]
        ).reshape(8, ROWS, COLS)

    def finish(g):
        for c in range(g * 8, g * 8 + 8):
            for s in range(ROWS // SLAB):
                x = slice(s * SLAB, s * SLAB + SLAB)
                value = linear[c, x] + bias[c]
                cdf = 0.5 + 0.5 * lax.erf(value * (1.0 / math.sqrt(2.0)))
                density = jnp.exp(-0.5 * value * value) * (1.0 / math.sqrt(2.0 * math.pi))
                slope[c, x] = (value * cdf).astype(BF16)
                seed[c, x] = (cotangent[c, x].astype(F32) * (cdf + value * density)).astype(BF16)
        to_columns(seed, g)
        send_parts(back_parts, back_comm, g)

    all_gather(tile, comm, lambda: reduce_scatter_sent(parts, comm), point, finish)
    plane_stage(back_parts, back_comm, GROUPS - 1)
    map_channels(mixer, seed, linear)
    cot = reduce_scatter(back_comm) * mode_weight()

    def meanwhile():
        weight_terms(spectrum, cot, weight_grad)
        reduce_scatter_sent(back_parts, back_comm)
        all_gather_sent(comm)

    all_gather(
        mix_back(weights, cot) * (1.0 / GRID),
        back_comm,
        meanwhile,
        lambda g: expand(back_comm[MODES], up[...], g, back_rows),
    )
    all_gather_sent(back_comm)


def final_kernel(
    slope, weight_grad, linear, rows, basis_t,
    slope_out, weight_grad_out, grad_out,
    grad, sems, done_sems,
):
    done = [
        pltpu.make_async_copy(slope, slope_out, done_sems.at[0]),
        pltpu.make_async_copy(weight_grad, weight_grad_out, done_sems.at[1]),
    ]
    for copy in done:
        copy.start()
    size = C * SLAB
    copies = []
    for s in range(ROWS // SLAB):
        at = pl.ds(s * SLAB, SLAB)
        value = linear[:, at, :].reshape(size, COLS) + dot(
            rows[:, at, :].reshape(size, 256), basis_t[...]
        )
        grad[:, at, :] = value.astype(BF16).reshape(C, SLAB, COLS)
        copy = pltpu.make_async_copy(grad.at[:, at, :], grad_out.at[:, at, :], sems.at[s])
        copy.start()
        copies.append(copy)
    for copy in copies + done:
        copy.wait()


VMEM = pl.BlockSpec(memory_space=pltpu.VMEM)
HBM = pl.BlockSpec(memory_space=pltpu.HBM)
SMEM = pl.BlockSpec(memory_space=pltpu.SMEM)


def params(megabytes, **more):
    return pltpu.CompilerParams(vmem_limit_bytes=megabytes * 1024 * 1024, **more)


def solution(mesh):
    basis_np, basis_t_np = column_tables()
    down_np, up_np = row_tables()

    def per_device(section_state, cotangent, bypass_weight, bias, spectral_weight):
        def in_hbm(array):
            return pltpu.with_memory_space_constraint(jnp.asarray(array), pltpu.HBM)

        tables = [in_hbm(table) for table in (basis_np, basis_t_np, down_np, up_np)]
        arguments = (
            section_state, cotangent, bypass_weight, bias, jnp.swapaxes(spectral_weight, 2, 3)
        )
        rows_shape = jax.ShapeDtypeStruct((C, ROWS, 256), BF16)
        field = jax.ShapeDtypeStruct((C, ROWS, COLS), BF16)
        modes_shape = jax.ShapeDtypeStruct((2, C, 16, C), F32)
        basis_shape = jax.ShapeDtypeStruct((256, COLS), BF16)
        wide_field = jax.ShapeDtypeStruct((C, ROWS, COLS), F32)

        slope, linear, rows, weight_grad, basis_t = pl.pallas_call(
            main_kernel,
            out_shape=(field, wide_field, rows_shape, modes_shape, basis_shape),
            in_specs=[HBM] * 9,
            out_specs=(VMEM,) * 5,
            scratch_shapes=[
                pltpu.VMEM((C, ROWS, COLS), BF16),
                pltpu.VMEM((C, ROWS, COLS), BF16),
                pltpu.VMEM((C, ROWS, COLS), BF16),
                pltpu.VMEM((C, ROWS, 256), BF16),
                pltpu.VMEM((C, ROWS, 256), F32),
                pltpu.VMEM((C, C), BF16),
                pltpu.SMEM((C,), F32),
                pltpu.VMEM((2, C, 16, C), F32),
                pltpu.VMEM((2, C, C, 16), F32),
                pltpu.VMEM((COLS, 256), BF16),
                pltpu.VMEM((128, 256), BF16),
                pltpu.VMEM((256, 192), BF16),
                pltpu.VMEM((C * SLAB, C * SLAB), BF16),
                pltpu.VMEM((C * SLAB, C * SLAB), BF16),
                pltpu.VMEM((GROUPS, 2, 256, 128), F32),
                pltpu.VMEM((GROUPS, 2, 256, 128), F32),
                pltpu.SemaphoreType.DMA((11,)),
                *COMM_SCRATCH,
                *COMM_SCRATCH,
            ],
            compiler_params=params(26, collective_id=0, has_side_effects=True),
            name="section",
        )(*(in_hbm(array) for array in arguments), *tables)

        slope, weight_grad, state_grad = pl.pallas_call(
            final_kernel,
            out_shape=(field, modes_shape, field),
            in_specs=[VMEM] * 5,
            out_specs=(HBM, HBM, HBM),
            scratch_shapes=[
                pltpu.VMEM((C, ROWS, COLS), BF16),
                pltpu.SemaphoreType.DMA((ROWS // SLAB,)),
                pltpu.SemaphoreType.DMA((2,)),
            ],
            compiler_params=params(16),
            name="state_gradient",
        )(slope, weight_grad, linear, rows, basis_t)
        return slope, state_grad, jnp.swapaxes(weight_grad, 2, 3)

    split_modes = P(None, None, None, ("wide", "narrow"))
    tiles = P(None, "wide", "narrow")
    return jax.shard_map(
        per_device,
        mesh=mesh,
        in_specs=(tiles, tiles, P(), P(), split_modes),
        out_specs=(tiles, tiles, split_modes),
        check_vma=False,
    )
```
